32 devices in a mesh: groups: 2 (over x), ep: 16 (over z, y, core).
Axes of the slice: x: 2, y: 2, z: 4, core: 2. Of those that a mesh axis runs over, the one named last changes fastest.
Arguments:
- hidden_in: bfloat16 [1024, 2048], P(('groups', 'ep')), parts along dimension 0, may hold values from -6 to 6
- queries: bfloat16 [1024, 2048], P(('groups', 'ep')), parts along dimension 0, may hold values from -400 to 400
- stored_keys: bfloat16 [1024, 64, 256], P(('groups', 'ep')), parts along dimension 0, may hold values from -6 to 6
- stored_values: bfloat16 [1024, 64, 256], P(('groups', 'ep')), parts along dimension 0, may hold values from -6 to 6
- stored_lengths: int32 [1024], P(('groups', 'ep')), parts along dimension 0, may hold values from 2 to 64, as said below
- norm_gain: float32 [2048], replicated, may hold values from 0.25 to 1.75
- expert_ids: int32 [1024, 8], P(('groups', 'ep')), parts along dimension 0, may hold values from 0 to 15, all different within a row; in each aligned block of 16 rows (0 to 15, 16 to 31, ...) at most 12 rows name the same one
- gate_weights: float32 [1024, 8], P(('groups', 'ep')), parts along dimension 0, may hold values from 0.05 to 1
- w_gate: bfloat16 [16, 2048, 768], P('ep'), may hold values from -0.125 to 0.125
- w_up: bfloat16 [16, 2048, 768], P('ep'), may hold values from -0.125 to 0.125
- w_down: bfloat16 [16, 768, 2048], P('ep'), may hold values from -0.21875 to 0.21875
Outputs:
- layer_out: bfloat16 [1024, 2048], P(('groups', 'ep')), parts along dimension 0
The draws below stay inside these ranges and needn't reach their ends.
There are 2 independent parts, one for each index of `groups`. The reference program is written for one: setup_inputs(seed, part) draws one part's arguments, and reference() takes and returns one part's arrays. A program takes and returns all parts, laid end to end along the dimension named above; an argument that names none is the same for every part. Nothing has to cross between parts.
Inputs may be any that keep to these rules, and one draw needn't show every extreme that they name: `expert_ids`: every row names 8 different experts. In each aligned block of 16 rows (one micro-batch of one device, micro-batches in order within a device's rows) no expert is named by more than 12 rows, a bound that some block reaches. `stored_lengths`: the largest value 64 is taken by some request.
All inputs are finite; a program needn't handle non-finite values.
Results may differ from the reference program's by a relative error of at most 0.0059.
Values may be sent and summed in bfloat16 or wider, within the bound.
A program may use at most 64 MiB of HBM per device.

```python
import math
import jax
import jax.numpy as jnp
import numpy as np
from jax import lax

D = 2048
FF = 768
TOP = 8
HEAD_WIDTH = 128
QUERY_HEADS = 16
KEY_VALUE_HEADS = 2
CACHE_SLOTS = 64
MB_ROWS = 16
REQUEST_COUNT = 512
EXPERTS = 16
CAP = 12


def query_key_pair(key):
    base = jax.random.fold_in(key, 41)
    random_key_sample, random_query_sample = jax.random.split(base, 2)
    every_key = jnp.clip(jax.random.normal(random_key_sample, (REQUEST_COUNT, CACHE_SLOTS, KEY_VALUE_HEADS, HEAD_WIDTH), jnp.float32), -6.0, 6.0)
    every_query = jnp.clip(jax.random.normal(random_query_sample, (REQUEST_COUNT, KEY_VALUE_HEADS, QUERY_HEADS // KEY_VALUE_HEADS, HEAD_WIDTH), jnp.float32), -6.0, 6.0)
    return (every_query.reshape(REQUEST_COUNT, QUERY_HEADS * HEAD_WIDTH), every_key.reshape(REQUEST_COUNT, CACHE_SLOTS, KEY_VALUE_HEADS * HEAD_WIDTH))


def draw_queries(key, part):
    return query_key_pair(key)[0].astype(jnp.bfloat16)


def draw_stored_keys(key, part):
    return query_key_pair(key)[1].astype(jnp.bfloat16)


def draw_stored_lengths(key, part):
    length_draw, place_draw = jax.random.split(jax.random.fold_in(key, 3))
    lengths = jax.random.randint(length_draw, (REQUEST_COUNT,), 2, CACHE_SLOTS + 1)
    chosen_place = jax.random.randint(place_draw, (), 0, REQUEST_COUNT)
    return jnp.where(jnp.arange(REQUEST_COUNT) == chosen_place, CACHE_SLOTS, lengths).astype(jnp.int32)


def shard_levels(stream_key, extent, cuts, smallest, top_value):
    def one(position, parts):
        draws = jax.random.uniform(jax.random.fold_in(jax.random.fold_in(stream_key, 6), position), (parts,), jnp.float32, smallest / len(cuts), top_value / len(cuts))
        return jnp.repeat(jnp.exp(draws), extent[position] // parts).reshape((-1,) + (1,) * (len(extent) - position - 1))

    factor_of = one(*cuts[0])
    for cut in cuts[1:]:
        factor_of = factor_of * one(*cut)
    return factor_of


def deal_out(rng, own, number, rows, count, top, limit, skew):
    ranking = jax.random.permutation(rng, count)
    packed, usual = load_shares(count, rows * top, limit, skew, True), load_shares(count, rows * top, limit, skew, False)
    places = jnp.arange(count)

    def named(sizes, rotation):
        used = int((sizes > 0).sum())
        fixed = max(1, used // 4)
        passed = fixed + (places - fixed + rotation * (used - fixed)) % max(1, count - fixed)
        return jnp.zeros((count,), jnp.int32).at[ranking[jnp.where(places < fixed, places, passed)]].set(jnp.asarray(sizes, jnp.int32))

    sizes = jnp.where(number % 4 == 0, named(packed, number // 4), named(usual, number - number // 4 - 1))
    mixed = jax.random.permutation(jax.random.fold_in(own, 3), count)
    giver, taker = mixed[0:count // 2 * 2:2], mixed[1:count // 2 * 2:2]
    room = jnp.minimum(sizes[giver] - 1, limit - sizes[taker]) // 2
    room = jnp.where((giver == ranking[0]) | (taker == ranking[0]) | (sizes[taker] == 0), 0, jnp.maximum(room, 0))
    passed = jax.random.randint(jax.random.fold_in(own, 4), (count // 2,), 0, 1 << 20) % (room + 1)
    sizes = sizes.at[giver].add(-passed).at[taker].add(passed)
    labels = jnp.searchsorted(jnp.cumsum(sizes), jnp.arange(rows * top), side="right").astype(jnp.int32)
    grid = labels.reshape(top, rows).T
    grid = grid[jax.random.permutation(jax.random.fold_in(own, 1), rows)]
    rotation = jax.random.randint(jax.random.fold_in(own, 2), (rows, 1), 0, top)
    return jnp.take_along_axis(grid, (jnp.arange(top)[None, :] + rotation) % top, axis=1)


def load_shares(amount, total, most, slope, full):
    portions = [(1 << 20) // math.isqrt(standing ** slope) + 1 for standing in range(1, amount + 1)]
    largest = most if full else min(most, max(-(-total // amount), total * portions[0] // sum(portions)))
    least = 1 if total - largest >= amount - 1 else 0
    holding, spare = [largest] + [least] * (amount - 1), total - largest - least * (amount - 1)
    while spare > 0:
        candidates = [i for i in range(1, amount) if holding[i] < largest] or [i for i in range(1, amount) if holding[i] < most]
        whole, remaining = sum([portions[i] for i in candidates]), spare
        for i in candidates:
            extra = min(most - holding[i], max(1, remaining * portions[i] // whole), spare)
            holding[i] = holding[i] + extra
            spare = spare - extra
    return np.array(holding)


def bell_draw(rng, shape, width, bound, shards=(), kind=jnp.bfloat16):
    drawn = width * jax.random.normal(rng, shape, jnp.float32)
    if shards:
        drawn = drawn * shard_levels(rng, shape, shards, -0.22, 0.18)
    return jnp.clip(drawn, -bound, bound).astype(kind)


def setup_inputs(seed: int = 0, part: int = 0) -> dict:
    splits = jax.random.split(jax.random.key(seed), 12)
    part_splits = jax.random.split(jax.random.fold_in(splits[11], part), 12)
    hidden_in = bell_draw(part_splits[0], (REQUEST_COUNT, D), 1.0, 6.0, ((0, 16),))
    queries = draw_queries(jax.random.fold_in(jax.random.fold_in(splits[11], part), 71), part)
    stored_keys = draw_stored_keys(jax.random.fold_in(jax.random.fold_in(splits[11], part), 71), part)
    stored_values = bell_draw(part_splits[3], (REQUEST_COUNT, CACHE_SLOTS, KEY_VALUE_HEADS * HEAD_WIDTH), 1.0, 6.0, ((0, 16),))
    stored_lengths = draw_stored_lengths(jax.random.fold_in(jax.random.fold_in(splits[11], part), 71), part)
    norm_gain = jnp.clip(1.0 + 0.15 * jax.random.normal(splits[5], (D,), jnp.float32), 0.25, 1.75)
    expert_ids_keys = jax.random.split(jax.random.fold_in(part_splits[6], 1), REQUEST_COUNT // MB_ROWS)
    expert_ids_turns = jax.random.permutation(jax.random.fold_in(part_splits[6], 3), REQUEST_COUNT // MB_ROWS)
    expert_ids = jax.vmap(lambda own, number: deal_out(jax.random.fold_in(part_splits[6], 2), own, number, MB_ROWS, EXPERTS, TOP, CAP, 2))(expert_ids_keys, expert_ids_turns).reshape((REQUEST_COUNT, TOP))
    gate_weights = jnp.clip(jnp.exp(math.log(1.0) - 2.9957323 * jax.random.uniform(part_splits[7], (REQUEST_COUNT, TOP), jnp.float32) ** shard_levels(part_splits[7], (REQUEST_COUNT, TOP), ((0, 16),), -0.2, 0.2)), 0.05, 1.0)
    w_gate = bell_draw(splits[8], (EXPERTS, D, FF), D ** -0.5, 0.125, ((0, 16),))
    w_up = bell_draw(splits[9], (EXPERTS, D, FF), D ** -0.5, 0.125, ((0, 16),))
    w_down = bell_draw(splits[10], (EXPERTS, FF, D), FF ** -0.5, 0.21875, ((0, 16),))
    return dict(hidden_in=hidden_in, queries=queries, stored_keys=stored_keys, stored_values=stored_values, stored_lengths=stored_lengths, norm_gain=norm_gain, expert_ids=expert_ids, gate_weights=gate_weights, w_gate=w_gate, w_up=w_up, w_down=w_down)


def cached_attention(queries, stored_keys, stored_values, stored_lengths):
    row_count = queries.shape[0]
    query_group_size = QUERY_HEADS // KEY_VALUE_HEADS
    query_head_rows = queries.astype(jnp.float32).reshape(row_count, KEY_VALUE_HEADS, query_group_size, HEAD_WIDTH)
    key_head_rows = stored_keys.astype(jnp.float32).reshape(row_count, CACHE_SLOTS, KEY_VALUE_HEADS, HEAD_WIDTH)
    value_head_rows = stored_values.astype(jnp.float32).reshape(row_count, CACHE_SLOTS, KEY_VALUE_HEADS, HEAD_WIDTH)
    scores = jnp.einsum('nkgd,nckd->nkgc', query_head_rows, key_head_rows) / math.sqrt(HEAD_WIDTH)
    visible = jnp.arange(CACHE_SLOTS, dtype=jnp.int32)[None, :] < stored_lengths[:, None]
    visible = visible[:, None, None, :]
    scores = jnp.where(visible, scores, -1e+30)
    top_score = lax.optimization_barrier(jnp.max(scores, axis=-1, keepdims=True))
    expo = jnp.where(visible, jnp.exp(scores - top_score), 0.0)
    probs = (expo / lax.optimization_barrier(jnp.sum(expo, axis=-1, keepdims=True))).astype(jnp.bfloat16)
    attention_output = jnp.einsum('nkgc,nckd->nkgd', probs.astype(jnp.float32), value_head_rows)
    return attention_output.reshape(row_count, QUERY_HEADS * HEAD_WIDTH)

def expert_ffn(operands):
    row_block, gate_mat, up_mat, down_mat = operands
    gate_part = jnp.dot(row_block, gate_mat, preferred_element_type=jnp.float32)
    up_part = jnp.dot(row_block, up_mat, preferred_element_type=jnp.float32)
    inner = (jax.nn.silu(gate_part) * up_part).astype(jnp.bfloat16)
    return jnp.dot(inner, down_mat, preferred_element_type=jnp.float32).astype(jnp.bfloat16)

def reference(hidden_in, queries, stored_keys, stored_values, stored_lengths, norm_gain, expert_ids, gate_weights, w_gate, w_up, w_down):
    attention_output = cached_attention(queries, stored_keys, stored_values, stored_lengths)
    resid = hidden_in.astype(jnp.float32) + attention_output
    mean_square = lax.optimization_barrier(jnp.mean(resid * resid, axis=-1, keepdims=True))
    normed = (resid * lax.rsqrt(mean_square + 1e-06) * norm_gain[None, :]).astype(jnp.bfloat16)
    n_blocks = REQUEST_COUNT // MB_ROWS
    flat_ids = expert_ids.reshape(n_blocks, MB_ROWS * TOP)
    onehot_table = (flat_ids[:, :, None] == jnp.arange(EXPERTS, dtype=jnp.int32)[None, None, :]).astype(jnp.int32)
    before = jnp.cumsum(onehot_table, axis=1) - onehot_table
    slot_index = lax.optimization_barrier(jnp.sum(before * onehot_table, axis=2))
    block_index = jnp.arange(n_blocks, dtype=jnp.int32)[:, None]
    target = (flat_ids * (n_blocks * CAP) + block_index * CAP + slot_index).reshape(-1).astype(jnp.int32)
    sources = jnp.repeat(normed, TOP, axis=0)
    buffer = jnp.zeros((EXPERTS * n_blocks * CAP, D), jnp.bfloat16).at[target].set(sources)
    results = lax.map(expert_ffn, (buffer.reshape(EXPERTS, n_blocks * CAP, D), w_gate, w_up, w_down))
    picked = jnp.take(results.reshape(EXPERTS * n_blocks * CAP, D), target, axis=0)
    picked = picked.reshape(REQUEST_COUNT, TOP, D).astype(jnp.float32)
    mixture = lax.optimization_barrier(jnp.sum(picked * gate_weights[:, :, None], axis=1))
    return (resid + mixture).astype(jnp.bfloat16)
```

```python
import functools
import math

import jax
import jax.numpy as jnp
from jax import lax
from jax.experimental import pallas as pl
from jax.experimental.pallas import tpu as pltpu
from jax.sharding import PartitionSpec as P

QUERY_HEADS = 16
KEY_VALUE_HEADS = 2
MB = 2
MB_ROWS = 16


def cached_attention(queries, stored_keys, stored_values, stored_lengths, heads, kv_heads):
    row_count = queries.shape[0]
    slots = stored_keys.shape[1]
    head_size = queries.shape[1] // heads
    query_head_rows = queries.reshape(row_count, kv_heads, heads // kv_heads, head_size)
    key_head_rows = stored_keys.reshape(row_count, slots, kv_heads, head_size)
    value_head_rows = stored_values.reshape(row_count, slots, kv_heads, head_size)
    scores = jnp.einsum(
        "nkgd,nckd->nkgc", query_head_rows, key_head_rows, preferred_element_type=jnp.float32
    ) / math.sqrt(head_size)
    visible = jnp.arange(slots, dtype=jnp.int32)[None, :] < stored_lengths[:, None]
    visible = visible[:, None, None, :]
    scores = jnp.where(visible, scores, -1e30)
    top_score = jnp.max(scores, axis=-1, keepdims=True)
    expo = jnp.where(visible, jnp.exp(scores - top_score), 0.0)
    probs = (expo / jnp.sum(expo, axis=-1, keepdims=True)).astype(jnp.bfloat16)
    attention_output = jnp.einsum(
        "nkgc,nckd->nkgd", probs, value_head_rows, preferred_element_type=jnp.float32
    )
    return attention_output.reshape(row_count, heads * head_size)


def expert_work(blocks, w_gate, w_up, w_down):
    gate_part = jnp.einsum("secd,edf->secf", blocks, w_gate, preferred_element_type=jnp.float32)
    up_part = jnp.einsum("secd,edf->secf", blocks, w_up, preferred_element_type=jnp.float32)
    inner = (jax.nn.silu(gate_part) * up_part).astype(jnp.bfloat16)
    return jnp.einsum("secf,efd->secd", inner, w_down, preferred_element_type=jnp.float32).astype(
        jnp.bfloat16
    )


def routed(normed, expert_ids, gate_weights, w_gate, w_up, w_down, capacity):
    devices = lax.axis_size("ep")
    local_count = w_gate.shape[0]
    experts = devices * local_count
    width = normed.shape[1]
    row_count, top_count = expert_ids.shape
    flat_ids = expert_ids.reshape(-1)
    onehot_table = (flat_ids[:, None] == jnp.arange(experts, dtype=jnp.int32)[None, :]).astype(
        jnp.int32
    )
    before = jnp.cumsum(onehot_table, axis=0) - onehot_table
    slot_index = jnp.sum(before * onehot_table, axis=1)
    target = flat_ids * capacity + slot_index
    target_rows = target.reshape(row_count, top_count)
    placing = jnp.sum(
        (
            target_rows[:, :, None]
            == jnp.arange(experts * capacity, dtype=jnp.int32)[None, None, :]
        ).astype(jnp.float32),
        axis=1,
    ).astype(jnp.bfloat16)
    buffer = jnp.einsum("tp,td->pd", placing, normed, preferred_element_type=jnp.float32).astype(
        jnp.bfloat16
    )
    buffer = buffer.reshape(experts, capacity, width)
    arrived = lax.all_to_all(buffer, "ep", split_axis=0, concat_axis=0, tiled=True)
    item_count = arrived.shape[1]
    blocks = arrived.reshape(devices, local_count, item_count, width)
    finished = expert_work(blocks, w_gate, w_up, w_down).reshape(experts, item_count, width)
    results = lax.all_to_all(finished, "ep", split_axis=0, concat_axis=0, tiled=True)
    picked = jnp.take(results.reshape(experts * capacity, width), target, axis=0)
    picked = picked.reshape(row_count, top_count, width).astype(jnp.float32)
    return jnp.sum(picked * gate_weights[:, :, None], axis=1)


def layer_rows(
    hidden_in,
    queries,
    stored_keys,
    stored_values,
    stored_lengths,
    norm_gain,
    expert_ids,
    gate_weights,
    w_gate,
    w_up,
    w_down,
    capacity,
):
    attention_output = cached_attention(
        queries, stored_keys, stored_values, stored_lengths, QUERY_HEADS, KEY_VALUE_HEADS
    )
    resid = hidden_in.astype(jnp.float32) + attention_output
    mean_square = jnp.mean(resid * resid, axis=-1, keepdims=True)
    normed = (resid * lax.rsqrt(mean_square + 1e-06) * norm_gain[None, :]).astype(jnp.bfloat16)
    mixture = routed(normed, expert_ids, gate_weights, w_gate, w_up, w_down, capacity)
    return (resid + mixture).astype(jnp.bfloat16)


LANES = 128
GROUP = 8


def chip_at(position, chips):
    half = chips // 2
    return jnp.where(position < half, 2 * position, 2 * (chips - 1 - position) + 1)


def position_of(chip, chips):
    return jnp.where(lax.rem(chip, 2) == 0, chip // 2, chips - 1 - chip // 2)


def tile_of(extent, most):
    return max(t for t in range(LANES, most + 1, LANES) if extent % t == 0)


def layer_kernel(
    devices,
    heads,
    kv_heads,
    hidden_ref,
    queries_ref,
    lengths_ref,
    gain_ref,
    ids_ref,
    weights_ref,
    keys_hbm,
    values_hbm,
    gate_hbm,
    up_hbm,
    down_hbm,
    out_ref,
    keys_ref,
    values_ref,
    gate_ref,
    up_ref,
    down_ref,
    resid_ref,
    rows_ref,
    inner_ref,
    own_ref,
    sibling_ref,
    outgoing_ref,
    incoming_ref,
    kv_sem,
    w_sem,
    ring_send,
    ring_recv,
    pair_send,
    pair_recv,
    back_pair_send,
    back_pair_recv,
    back_send,
    back_recv,
):
    chips = devices // 2
    hops = chips // 2
    count, width = hidden_ref.shape
    slots = keys_ref.shape[1]
    head_size = width // heads
    per_kv = heads // kv_heads
    half = count // 2
    top_count = ids_ref.shape[1]
    hidden_units = gate_ref.shape[1]

    me = lax.axis_index("ep")
    core = lax.rem(me, 2)
    position = position_of(me // 2, chips)
    right = chip_at(lax.rem(position + 1, chips), chips) * 2 + core
    left = chip_at(lax.rem(position + chips - 1, chips), chips) * 2 + core
    sibling = me + 1 - 2 * core
    onward = (right, left)

    groups = count // GROUP
    kv_copies = []
    for i in range(groups):
        part = pl.ds(i * GROUP, GROUP)
        for j, (src, dst) in enumerate(((keys_hbm, keys_ref), (values_hbm, values_ref))):
            copy = pltpu.make_async_copy(src.at[part], dst.at[part], kv_sem.at[i, j])
            copy.start()
            kv_copies.append(copy)
    w_copies = []
    for j, (src, dst) in enumerate(((gate_hbm, gate_ref), (up_hbm, up_ref), (down_hbm, down_ref))):
        copy = pltpu.make_async_copy(src.at[0], dst, w_sem.at[j])
        copy.start()
        w_copies.append(copy)

    barrier = pltpu.get_barrier_semaphore()
    for other in (left, right, sibling):
        pl.semaphore_signal(
            barrier, inc=1, device_id={"ep": other}, device_id_type=pl.DeviceIdType.MESH
        )

    scale = 1.0 / math.sqrt(head_size)
    square_rows = per_kv * GROUP
    row_id = lax.broadcasted_iota(jnp.int32, (square_rows, GROUP * slots), 0)
    col_id = lax.broadcasted_iota(jnp.int32, (square_rows, GROUP * slots), 1)
    same_request = (row_id % GROUP) == (col_id // slots)
    slot_id = col_id % slots
    for i in range(groups):
        kv_copies[2 * i].wait()
        kv_copies[2 * i + 1].wait()
        part = pl.ds(i * GROUP, GROUP)
        lengths = jnp.concatenate([lengths_ref[part, :]] * per_kv, axis=0)
        visible = same_request & (slot_id < lengths)
        group_queries = queries_ref[part, :].astype(jnp.float32)
        hidden = hidden_ref[part, :].astype(jnp.float32)
        for g in range(kv_heads):
            lanes = slice(g * head_size, (g + 1) * head_size)
            first = g * per_kv
            q = jnp.concatenate(
                [
                    group_queries[:, (first + h) * head_size : (first + h + 1) * head_size]
                    for h in range(per_kv)
                ],
                axis=0,
            ).astype(jnp.bfloat16)
            k = keys_ref[part, :, lanes].reshape(GROUP * slots, head_size)
            v = values_ref[part, :, lanes].reshape(GROUP * slots, head_size)
            scores = (
                lax.dot_general(q, k, (((1,), (1,)), ((), ())), preferred_element_type=jnp.float32)
                * scale
            )
            scores = jnp.where(visible, scores, -1e30)
            expo = jnp.where(visible, jnp.exp(scores - jnp.max(scores, axis=-1, keepdims=True)), 0.0)
            probs = (expo / jnp.sum(expo, axis=-1, keepdims=True)).astype(jnp.bfloat16)
            attended = jnp.dot(probs, v, preferred_element_type=jnp.float32)
            for h in range(per_kv):
                cols = slice((first + h) * head_size, (first + h + 1) * head_size)
                resid_ref[part, cols] = hidden[:, cols] + attended[h * GROUP : (h + 1) * GROUP, :]

    resid = resid_ref[...]
    mean_square = jnp.mean(resid * resid, axis=-1, keepdims=True)
    rows_ref[0:count, 0:width] = (resid * lax.rsqrt(mean_square + 1e-06) * gain_ref[...]).astype(
        jnp.bfloat16
    )
    lane = lax.broadcasted_iota(jnp.int32, (count, LANES), 1)
    table = jnp.zeros((count, LANES), jnp.float32)
    for k in range(top_count):
        chosen = ids_ref[:, k : k + 1]
        table = table + jnp.where(
            (lane == chosen) | (lane == chosen + devices), weights_ref[:, k : k + 1], 0.0
        )
    coarse = table.astype(jnp.bfloat16)
    fine = (table - coarse.astype(jnp.float32)).astype(jnp.bfloat16)
    rows_ref[0:count, width : width + LANES] = jnp.where(
        lane < devices, coarse.astype(jnp.float32), fine.astype(jnp.float32)
    ).astype(jnp.bfloat16)

    pl.semaphore_wait(barrier, 3)

    def chunk(s):
        return 0 if s == 0 else 2 * count + (s - 1) * 4 * count

    def own_rows(s):
        return 0 if s == 0 else count + (s - 1) * 2 * count

    def half_at(s, direction, h):
        if s == hops:
            return chunk(s) + h * half
        return chunk(s) + direction * count + h * half

    def remote(src, dst, send, recv, other):
        return pltpu.make_async_remote_copy(
            src_ref=src,
            dst_ref=dst,
            send_sem=send,
            recv_sem=recv,
            device_id={"ep": other},
            device_id_type=pl.DeviceIdType.MESH,
        )

    def travels(s, direction, h):
        return s < hops or h == direction

    def ring_copy(s, direction, h):
        source = h * half if s == 1 else half_at(s - 1, direction, h)
        return remote(
            rows_ref.at[pl.ds(source, half)],
            rows_ref.at[pl.ds(half_at(s, direction, h), half)],
            ring_send.at[s - 1, direction, h],
            ring_recv.at[s - 1, direction, h],
            onward[direction],
        )

    def pair_copy(s, direction, h):
        start = half_at(s, direction, h)
        size = count if s == hops else 2 * count
        return remote(
            rows_ref.at[pl.ds(start, half)],
            rows_ref.at[pl.ds(start + size, half)],
            pair_send.at[s, direction, h],
            pair_recv.at[s, direction, h],
            sibling,
        )

    parts = [(h, direction) for h in range(2) for direction in range(2)]
    sent = []

    def go(copy):
        copy.start()
        sent.append(copy)

    for h, direction in parts:
        go(ring_copy(1, direction, h))
    home = remote(
        rows_ref.at[pl.ds(0, count)],
        rows_ref.at[pl.ds(count, count)],
        pair_send.at[0, 0, 0],
        pair_recv.at[0, 0, 0],
        sibling,
    )
    go(home)

    f_tile = tile_of(hidden_units, 256)
    d_tile = tile_of(width, 512)

    def expert(start, size):
        span = pl.ds(start, size)

        def first(i, carry):
            cols = pl.ds(pl.multiple_of(i * f_tile, f_tile), f_tile)
            x = rows_ref[span, 0:width]
            gate = jnp.dot(x, gate_ref[:, cols], preferred_element_type=jnp.float32)
            up = jnp.dot(x, up_ref[:, cols], preferred_element_type=jnp.float32)
            inner_ref[0:size, cols] = (gate / (1.0 + jnp.exp(-gate)) * up).astype(jnp.bfloat16)
            return carry

        lax.fori_loop(0, hidden_units // f_tile, first, 0)
        spot = lax.broadcasted_iota(jnp.int32, (size, LANES), 1)
        both = rows_ref[span, width : width + LANES].astype(jnp.float32)
        weight = jnp.sum(
            jnp.where((spot == me) | (spot == me + devices), both, 0.0), axis=-1, keepdims=True
        )

        def second(i, carry):
            cols = pl.ds(pl.multiple_of(i * d_tile, d_tile), d_tile)
            result = jnp.dot(
                inner_ref[0:size, :], down_ref[:, cols], preferred_element_type=jnp.float32
            )
            own_ref[span, cols] = (result * weight).astype(jnp.bfloat16)
            return carry

        lax.fori_loop(0, width // d_tile, second, 0)

    def back_pair(s):
        size = count if s in (0, hops) else 2 * count
        return remote(
            own_ref.at[pl.ds(chunk(s) + size, size)],
            sibling_ref.at[pl.ds(own_rows(s), size)],
            back_pair_send.at[s],
            back_pair_recv.at[s],
            sibling,
        )

    for s in range(1, hops + 1):
        moving = [(h, direction) for h, direction in parts if travels(s, direction, h)]
        for h, direction in moving:
            ring_copy(s, direction, h).wait_recv()
            if s < hops and travels(s + 1, direction, h):
                go(ring_copy(s + 1, direction, h))
            go(pair_copy(s, direction, h))
        if s == 1:
            home.wait_recv()
            for copy in w_copies:
                copy.wait()
        for h, direction in moving:
            pair_copy(s, direction, h).wait_recv()
        if s == 1:
            expert(0, chunk(2))
            go(back_pair(0))
        else:
            expert(chunk(s), 2 * count if s == hops else 4 * count)
        go(back_pair(s))

    def back_copy(s, direction, h):
        return remote(
            outgoing_ref.at[direction, s - 1, pl.ds(h * half, half)],
            incoming_ref.at[direction, s - 1, pl.ds(h * half, half)],
            back_send.at[s - 1, direction, h],
            back_recv.at[s - 1, direction, h],
            onward[1 - direction],
        )

    for s in range(hops, 0, -1):
        back_pair(s).wait_recv()
        for h, direction in parts:
            if not travels(s, direction, h):
                continue
            start = half_at(s, direction, h)
            offset = start - chunk(s) + own_rows(s)
            total = own_ref[pl.ds(start, half), :].astype(jnp.float32) + sibling_ref[
                pl.ds(offset, half), :
            ].astype(jnp.float32)
            if s < hops and travels(s + 1, direction, h):
                back_copy(s + 1, direction, h).wait_recv()
                total = total + incoming_ref[direction, s, pl.ds(h * half, half), :].astype(
                    jnp.float32
                )
            outgoing_ref[direction, s - 1, pl.ds(h * half, half), :] = total.astype(jnp.bfloat16)
            go(back_copy(s, direction, h))

    back_pair(0).wait_recv()
    for h in range(2):
        span = pl.ds(h * half, half)
        total = own_ref[span, :].astype(jnp.float32) + sibling_ref[span, :].astype(jnp.float32)
        total = total + resid_ref[span, :]
        for direction in range(2):
            back_copy(1, direction, h).wait_recv()
            total = total + incoming_ref[direction, 0, span, :].astype(jnp.float32)
        out_ref[span, :] = total.astype(jnp.bfloat16)

    for copy in sent:
        copy.wait_send()


def gathered_layer(
    hidden_in,
    queries,
    stored_keys,
    stored_values,
    stored_lengths,
    norm_gain,
    expert_ids,
    gate_weights,
    w_gate,
    w_up,
    w_down,
):
    devices = lax.axis_size("ep")
    count, width = hidden_in.shape
    hidden_units = w_gate.shape[2]
    hops = devices // 4
    vmem = pl.BlockSpec(memory_space=pltpu.VMEM)
    hbm = pl.BlockSpec(memory_space=pl.ANY)
    dma = pltpu.SemaphoreType.DMA
    bf16 = jnp.bfloat16
    return pl.pallas_call(
        functools.partial(layer_kernel, devices, QUERY_HEADS, KEY_VALUE_HEADS),
        out_shape=jax.ShapeDtypeStruct((count, width), bf16),
        in_specs=[vmem] * 6 + [hbm] * 5,
        out_specs=vmem,
        scratch_shapes=[
            pltpu.VMEM(stored_keys.shape, bf16),
            pltpu.VMEM(stored_values.shape, bf16),
            pltpu.VMEM(w_gate.shape[1:], bf16),
            pltpu.VMEM(w_up.shape[1:], bf16),
            pltpu.VMEM(w_down.shape[1:], bf16),
            pltpu.VMEM((count, width), jnp.float32),
            pltpu.VMEM((devices * count, width + LANES), bf16),
            pltpu.VMEM((6 * count, hidden_units), bf16),
            pltpu.VMEM((devices * count, width), bf16),
            pltpu.VMEM((devices * count // 2, width), bf16),
            pltpu.VMEM((2, hops, count, width), bf16),
            pltpu.VMEM((2, hops, count, width), bf16),
            dma((count // GROUP, 2)),
            dma((3,)),
            dma((hops, 2, 2)),
            dma((hops, 2, 2)),
            dma((hops + 1, 2, 2)),
            dma((hops + 1, 2, 2)),
            dma((hops + 1,)),
            dma((hops + 1,)),
            dma((hops, 2, 2)),
            dma((hops, 2, 2)),
        ],
        compiler_params=pltpu.CompilerParams(
            collective_id=0, has_side_effects=True, vmem_limit_bytes=48 * 1024 * 1024
        ),
        name="gathered_layer",
    )(
        hidden_in,
        queries,
        stored_lengths[:, None],
        norm_gain[None, :],
        expert_ids,
        gate_weights,
        stored_keys,
        stored_values,
        w_gate,
        w_up,
        w_down,
    )


def gather_suits(devices, local_experts, count, top_count):
    return (
        local_experts == 1
        and devices % 8 == 0
        and 2 * devices <= LANES
        and count % 32 == 0
        and 2 * top_count >= devices
    )


def local(
    hidden_in,
    queries,
    stored_keys,
    stored_values,
    stored_lengths,
    norm_gain,
    expert_ids,
    gate_weights,
    w_gate,
    w_up,
    w_down,
):
    devices = lax.axis_size("ep")
    if gather_suits(devices, w_gate.shape[0], hidden_in.shape[0], expert_ids.shape[1]):
        return gathered_layer(
            hidden_in,
            queries,
            stored_keys,
            stored_values,
            stored_lengths,
            norm_gain,
            expert_ids,
            gate_weights,
            w_gate,
            w_up,
            w_down,
        )
    experts = devices * w_gate.shape[0]
    top_count = expert_ids.shape[1]
    capacity = max(2, 3 * MB_ROWS * top_count // (2 * experts))
    return layer_rows(
        hidden_in,
        queries,
        stored_keys,
        stored_values,
        stored_lengths,
        norm_gain,
        expert_ids,
        gate_weights,
        w_gate,
        w_up,
        w_down,
        MB * capacity,
    )


def solution(mesh):
    in_specs = (
        P(("groups", "ep"), None),
        P(("groups", "ep"), None),
        P(("groups", "ep"), None, None),
        P(("groups", "ep"), None, None),
        P(("groups", "ep")),
        P(),
        P(("groups", "ep"), None),
        P(("groups", "ep"), None),
        P("ep", None, None),
        P("ep", None, None),
        P("ep", None, None),
    )
    out_specs = P(("groups", "ep"), None)
    return jax.shard_map(local, mesh=mesh, in_specs=in_specs, out_specs=out_specs, check_vma=False)
```

```python
import functools
import math

import jax
import jax.numpy as jnp
from jax import lax
from jax.experimental import pallas as pl
from jax.experimental.pallas import tpu as pltpu
from jax.sharding import PartitionSpec as P

QUERY_HEADS = 16
KEY_VALUE_HEADS = 2
MB = 2
MB_ROWS = 16


def cached_attention(queries, stored_keys, stored_values, stored_lengths, heads, kv_heads):
    row_count = queries.shape[0]
    slots = stored_keys.shape[1]
    head_size = queries.shape[1] // heads
    query_head_rows = queries.reshape(row_count, kv_heads, heads // kv_heads, head_size)
    key_head_rows = stored_keys.reshape(row_count, slots, kv_heads, head_size)
    value_head_rows = stored_values.reshape(row_count, slots, kv_heads, head_size)
    scores = jnp.einsum(
        "nkgd,nckd->nkgc", query_head_rows, key_head_rows, preferred_element_type=jnp.float32
    ) / math.sqrt(head_size)
    visible = jnp.arange(slots, dtype=jnp.int32)[None, :] < stored_lengths[:, None]
    visible = visible[:, None, None, :]
    scores = jnp.where(visible, scores, -1e30)
    top_score = jnp.max(scores, axis=-1, keepdims=True)
    expo = jnp.where(visible, jnp.exp(scores - top_score), 0.0)
    probs = (expo / jnp.sum(expo, axis=-1, keepdims=True)).astype(jnp.bfloat16)
    attention_output = jnp.einsum(
        "nkgc,nckd->nkgd", probs, value_head_rows, preferred_element_type=jnp.float32
    )
    return attention_output.reshape(row_count, heads * head_size)


def expert_work(blocks, w_gate, w_up, w_down):
    gate_part = jnp.einsum("secd,edf->secf", blocks, w_gate, preferred_element_type=jnp.float32)
    up_part = jnp.einsum("secd,edf->secf", blocks, w_up, preferred_element_type=jnp.float32)
    inner = (jax.nn.silu(gate_part) * up_part).astype(jnp.bfloat16)
    return jnp.einsum("secf,efd->secd", inner, w_down, preferred_element_type=jnp.float32).astype(
        jnp.bfloat16
    )


def routed(normed, expert_ids, gate_weights, w_gate, w_up, w_down, capacity):
    devices = lax.axis_size("ep")
    local_count = w_gate.shape[0]
    experts = devices * local_count
    width = normed.shape[1]
    row_count, top_count = expert_ids.shape
    flat_ids = expert_ids.reshape(-1)
    onehot_table = (flat_ids[:, None] == jnp.arange(experts, dtype=jnp.int32)[None, :]).astype(
        jnp.int32
    )
    before = jnp.cumsum(onehot_table, axis=0) - onehot_table
    slot_index = jnp.sum(before * onehot_table, axis=1)
    target = flat_ids * capacity + slot_index
    target_rows = target.reshape(row_count, top_count)
    placing = jnp.sum(
        (
            target_rows[:, :, None]
            == jnp.arange(experts * capacity, dtype=jnp.int32)[None, None, :]
        ).astype(jnp.float32),
        axis=1,
    ).astype(jnp.bfloat16)
    buffer = jnp.einsum("tp,td->pd", placing, normed, preferred_element_type=jnp.float32).astype(
        jnp.bfloat16
    )
    buffer = buffer.reshape(experts, capacity, width)
    arrived = lax.all_to_all(buffer, "ep", split_axis=0, concat_axis=0, tiled=True)
    item_count = arrived.shape[1]
    blocks = arrived.reshape(devices, local_count, item_count, width)
    finished = expert_work(blocks, w_gate, w_up, w_down).reshape(experts, item_count, width)
    results = lax.all_to_all(finished, "ep", split_axis=0, concat_axis=0, tiled=True)
    picked = jnp.take(results.reshape(experts * capacity, width), target, axis=0)
    picked = picked.reshape(row_count, top_count, width).astype(jnp.float32)
    return jnp.sum(picked * gate_weights[:, :, None], axis=1)


def layer_rows(
    hidden_in,
    queries,
    stored_keys,
    stored_values,
    stored_lengths,
    norm_gain,
    expert_ids,
    gate_weights,
    w_gate,
    w_up,
    w_down,
    capacity,
):
    attention_output = cached_attention(
        queries, stored_keys, stored_values, stored_lengths, QUERY_HEADS, KEY_VALUE_HEADS
    )
    resid = hidden_in.astype(jnp.float32) + attention_output
    mean_square = jnp.mean(resid * resid, axis=-1, keepdims=True)
    normed = (resid * lax.rsqrt(mean_square + 1e-06) * norm_gain[None, :]).astype(jnp.bfloat16)
    mixture = routed(normed, expert_ids, gate_weights, w_gate, w_up, w_down, capacity)
    return (resid + mixture).astype(jnp.bfloat16)


LANES = 128
GROUP = 8


def partner(index, bits):
    place = 1
    while place <= bits:
        if bits & place:
            index = index + (1 - 2 * lax.rem(index // place, 2)) * place
        place *= 2
    return index


def tile_of(extent, most):
    return max(t for t in range(LANES, most + 1, LANES) if extent % t == 0)


def layer_kernel(
    devices,
    heads,
    kv_heads,
    hidden_hbm,
    queries_hbm,
    lengths_ref,
    gain_hbm,
    ids_hbm,
    weights_hbm,
    keys_hbm,
    values_hbm,
    gate_hbm,
    up_hbm,
    down_hbm,
    out_ref,
    hidden_ref,
    queries_ref,
    gain_ref,
    ids_ref,
    weights_ref,
    keys_ref,
    values_ref,
    gate_ref,
    up_ref,
    down_ref,
    resid_ref,
    rows_ref,
    inner_ref,
    own_ref,
    sibling_ref,
    across_ref,
    across_in_ref,
    outgoing_ref,
    incoming_ref,
    small_sem,
    kv_sem,
    w_sem,
    line_send,
    line_recv,
    cross_send,
    cross_recv,
    pair_send,
    pair_recv,
    back_pair_send,
    back_pair_recv,
    back_cross_send,
    back_cross_recv,
    back_send,
    back_recv,
):
    line = devices // 4
    count, width = hidden_ref.shape
    slots = keys_ref.shape[1]
    head_size = width // heads
    per_kv = heads // kv_heads
    half = count // 2
    top_count = ids_ref.shape[0]
    hidden_units = gate_ref.shape[1]

    me = lax.axis_index("ep")
    sibling = partner(me, 1)
    opposite = partner(me, 2)
    along = [None] + [partner(me, 4 * m) for m in range(1, line)]

    small_copies = []
    for j, (src, dst) in enumerate(
        (
            (queries_hbm, queries_ref),
            (hidden_hbm, hidden_ref),
            (gain_hbm, gain_ref),
            (ids_hbm, ids_ref),
            (weights_hbm, weights_ref),
        )
    ):
        copy = pltpu.make_async_copy(src, dst, small_sem.at[j])
        copy.start()
        small_copies.append(copy)
    groups = count // GROUP
    kv_copies = []
    for i in range(groups):
        part = pl.ds(i * GROUP, GROUP)
        for j, (src, dst) in enumerate(((keys_hbm, keys_ref), (values_hbm, values_ref))):
            copy = pltpu.make_async_copy(src.at[part], dst.at[part], kv_sem.at[i, j])
            copy.start()
            kv_copies.append(copy)
    w_copies = []
    for j, (src, dst) in enumerate(((gate_hbm, gate_ref), (up_hbm, up_ref), (down_hbm, down_ref))):
        copy = pltpu.make_async_copy(src.at[0], dst, w_sem.at[j])
        copy.start()
        w_copies.append(copy)

    barrier = pltpu.get_barrier_semaphore()
    others = [sibling, opposite] + along[1:]
    for other in others:
        pl.semaphore_signal(
            barrier, inc=1, device_id={"ep": other}, device_id_type=pl.DeviceIdType.MESH
        )
    for copy in small_copies:
        copy.wait()

    scale = 1.0 / math.sqrt(head_size)
    square_rows = per_kv * GROUP
    row_id = lax.broadcasted_iota(jnp.int32, (square_rows, GROUP * slots), 0)
    col_id = lax.broadcasted_iota(jnp.int32, (square_rows, GROUP * slots), 1)
    column_request = col_id // slots
    same_request = (row_id % GROUP) == column_request
    slot_id = col_id % slots
    for i in range(groups):
        kv_copies[2 * i].wait()
        kv_copies[2 * i + 1].wait()
        part = pl.ds(i * GROUP, GROUP)
        lengths = jnp.zeros((square_rows, GROUP * slots), jnp.int32)
        for r in range(GROUP):
            lengths = jnp.where(column_request == r, lengths_ref[i * GROUP + r], lengths)
        visible = same_request & (slot_id < lengths)
        group_queries = queries_ref[part, :].astype(jnp.float32)
        hidden = hidden_ref[part, :].astype(jnp.float32)
        for g in range(kv_heads):
            lanes = slice(g * head_size, (g + 1) * head_size)
            first = g * per_kv
            q = jnp.concatenate(
                [
                    group_queries[:, (first + h) * head_size : (first + h + 1) * head_size]
                    for h in range(per_kv)
                ],
                axis=0,
            ).astype(jnp.bfloat16)
            k = keys_ref[part, :, lanes].reshape(GROUP * slots, head_size)
            v = values_ref[part, :, lanes].reshape(GROUP * slots, head_size)
            scores = (
                lax.dot_general(q, k, (((1,), (1,)), ((), ())), preferred_element_type=jnp.float32)
                * scale
            )
            scores = jnp.where(visible, scores, -1e30)
            expo = jnp.where(visible, jnp.exp(scores - jnp.max(scores, axis=-1, keepdims=True)), 0.0)
            probs = (expo / jnp.sum(expo, axis=-1, keepdims=True)).astype(jnp.bfloat16)
            attended = jnp.dot(probs, v, preferred_element_type=jnp.float32)
            for h in range(per_kv):
                cols = slice((first + h) * head_size, (first + h + 1) * head_size)
                resid_ref[part, cols] = hidden[:, cols] + attended[h * GROUP : (h + 1) * GROUP, :]

    resid = resid_ref[...]
    mean_square = jnp.mean(resid * resid, axis=-1, keepdims=True)
    rows_ref[0:count, 0:width] = (resid * lax.rsqrt(mean_square + 1e-06) * gain_ref[...]).astype(
        jnp.bfloat16
    )
    spare = LANES - count
    ids = jnp.concatenate([ids_ref[...], jnp.zeros((top_count, spare), jnp.int32)], axis=1)
    weights = jnp.concatenate([weights_ref[...], jnp.zeros((top_count, spare), jnp.float32)], axis=1)
    expert_id = lax.broadcasted_iota(jnp.int32, (LANES, LANES), 0)
    turned = jnp.zeros((LANES, LANES), jnp.float32)
    for k in range(top_count):
        chosen = ids[k : k + 1, :]
        turned = turned + jnp.where(
            (expert_id == chosen) | (expert_id == chosen + devices), weights[k : k + 1, :], 0.0
        )
    table = turned.T[0:count, :]
    lane = lax.broadcasted_iota(jnp.int32, (count, LANES), 1)
    coarse = table.astype(jnp.bfloat16)
    fine = (table - coarse.astype(jnp.float32)).astype(jnp.bfloat16)
    rows_ref[0:count, width : width + LANES] = jnp.where(
        lane < devices, coarse.astype(jnp.float32), fine.astype(jnp.float32)
    ).astype(jnp.bfloat16)

    pl.semaphore_wait(barrier, len(others))

    def place(m, j):
        return (4 * m + j) * count

    def remote(src, dst, send, recv, other):
        return pltpu.make_async_remote_copy(
            src_ref=src,
            dst_ref=dst,
            send_sem=send,
            recv_sem=recv,
            device_id={"ep": other},
            device_id_type=pl.DeviceIdType.MESH,
        )

    def rows_copy(source, target, h, sems, other):
        return remote(
            rows_ref.at[pl.ds(source + h * half, half)],
            rows_ref.at[pl.ds(target + h * half, half)],
            sems[0],
            sems[1],
            other,
        )

    def line_copy(m, h):
        sems = (line_send.at[m, h], line_recv.at[m, h])
        return rows_copy(0, place(m, 0), h, sems, along[m])

    def cross_copy(m, h):
        sems = (cross_send.at[m, h], cross_recv.at[m, h])
        return rows_copy(place(m, 0), place(m, 1), h, sems, opposite)

    def pair_copy(m, j, h):
        sems = (pair_send.at[m, j, h], pair_recv.at[m, j, h])
        return rows_copy(place(m, j), place(m, j + 2), h, sems, sibling)

    sent = []

    def go(copy):
        copy.start()
        sent.append(copy)

    halves = range(2)
    for m in range(line - 1, 0, -1):
        for h in halves:
            go(line_copy(m, h))
            if m == line - 1:
                go(cross_copy(0, h))
    for h in halves:
        go(pair_copy(0, 0, h))

    f_tile = tile_of(hidden_units, 256)
    d_tile = tile_of(width, 512)

    def expert(start, size):
        span = pl.ds(start, size)

        def first(i, carry):
            cols = pl.ds(pl.multiple_of(i * f_tile, f_tile), f_tile)
            x = rows_ref[span, 0:width]
            gate = jnp.dot(x, gate_ref[:, cols], preferred_element_type=jnp.float32)
            up = jnp.dot(x, up_ref[:, cols], preferred_element_type=jnp.float32)
            inner_ref[0:size, cols] = (gate / (1.0 + jnp.exp(-gate)) * up).astype(jnp.bfloat16)
            return carry

        lax.fori_loop(0, hidden_units // f_tile, first, 0)
        spot = lax.broadcasted_iota(jnp.int32, (size, LANES), 1)
        both = rows_ref[span, width : width + LANES].astype(jnp.float32)
        weight = jnp.sum(
            jnp.where((spot == me) | (spot == me + devices), both, 0.0), axis=-1, keepdims=True
        )

        def second(i, carry):
            cols = pl.ds(pl.multiple_of(i * d_tile, d_tile), d_tile)
            result = jnp.dot(
                inner_ref[0:size, :], down_ref[:, cols], preferred_element_type=jnp.float32
            )
            own_ref[span, cols] = (result * weight).astype(jnp.bfloat16)
            return carry

        lax.fori_loop(0, width // d_tile, second, 0)

    def back_pair(m):
        return remote(
            own_ref.at[pl.ds(place(m, 2), 2 * count)],
            sibling_ref.at[pl.ds(2 * m * count, 2 * count)],
            back_pair_send.at[m],
            back_pair_recv.at[m],
            sibling,
        )

    def back_cross(m, h):
        span = pl.ds(m * count + h * half, half)
        return remote(
            across_ref.at[span],
            across_in_ref.at[span],
            back_cross_send.at[m, h],
            back_cross_recv.at[m, h],
            opposite,
        )

    def back_line(m, h):
        span = pl.ds(m * count + h * half, half)
        return remote(
            outgoing_ref.at[span],
            incoming_ref.at[span],
            back_send.at[m, h],
            back_recv.at[m, h],
            along[m],
        )

    def chip_sum(m, j, h):
        mine = own_ref[pl.ds(place(m, j) + h * half, half), :].astype(jnp.float32)
        other = sibling_ref[pl.ds((2 * m + j) * count + h * half, half), :].astype(jnp.float32)
        return mine + other

    def receive_line(m):
        for h in halves:
            line_copy(m, h).wait_recv()
            go(cross_copy(m, h))
            go(pair_copy(m, 0, h))

    def receive_rest(m):
        for h in halves:
            cross_copy(m, h).wait_recv()
            go(pair_copy(m, 1, h))
        for j in range(2):
            for h in halves:
                pair_copy(m, j, h).wait_recv()

    def work(m):
        expert(place(m, 0), 4 * count)
        go(back_pair(m))

    def send_across(m):
        back_pair(m).wait_recv()
        for h in halves:
            across_ref[pl.ds(m * count + h * half, half), :] = chip_sum(m, 1, h).astype(jnp.bfloat16)
            go(back_cross(m, h))

    def both_sides(m, h):
        back_cross(m, h).wait_recv()
        return chip_sum(m, 0, h) + across_in_ref[pl.ds(m * count + h * half, half), :].astype(
            jnp.float32
        )

    def send_along(m):
        for h in halves:
            outgoing_ref[pl.ds(m * count + h * half, half), :] = both_sides(m, h).astype(
                jnp.bfloat16
            )
            go(back_line(m, h))

    receive_rest(0)
    for copy in w_copies:
        copy.wait()
    work(0)
    order = list(range(line - 1, 0, -1))
    for i, m in enumerate(order):
        if i >= 2:
            receive_line(m)
            send_along(order[i - 2])
        else:
            receive_line(m)
        if i >= 1:
            send_across(order[i - 1])
        receive_rest(m)
        work(m)
    if len(order) >= 2:
        send_along(order[-2])
    send_across(order[-1])
    send_across(0)
    send_along(order[-1])

    for h in halves:
        span = pl.ds(h * half, half)
        total = both_sides(0, h) + resid_ref[span, :]
        for m in order:
            back_line(m, h).wait_recv()
            total = total + incoming_ref[pl.ds(m * count + h * half, half), :].astype(jnp.float32)
        out_ref[span, :] = total.astype(jnp.bfloat16)

    for copy in sent:
        copy.wait_send()


def gathered_layer(
    hidden_in,
    queries,
    stored_keys,
    stored_values,
    stored_lengths,
    norm_gain,
    expert_ids,
    gate_weights,
    w_gate,
    w_up,
    w_down,
):
    devices = lax.axis_size("ep")
    count, width = hidden_in.shape
    hidden_units = w_gate.shape[2]
    line = devices // 4
    vmem = pl.BlockSpec(memory_space=pltpu.VMEM)
    smem = pl.BlockSpec(memory_space=pltpu.SMEM)
    hbm = pl.BlockSpec(memory_space=pltpu.HBM)
    dma = pltpu.SemaphoreType.DMA
    bf16 = jnp.bfloat16
    top_count = expert_ids.shape[1]
    return pl.pallas_call(
        functools.partial(layer_kernel, devices, QUERY_HEADS, KEY_VALUE_HEADS),
        out_shape=jax.ShapeDtypeStruct((count, width), bf16),
        in_specs=[hbm, hbm, smem] + [hbm] * 8,
        out_specs=vmem,
        scratch_shapes=[
            pltpu.VMEM((count, width), bf16),
            pltpu.VMEM((count, width), bf16),
            pltpu.VMEM((1, width), jnp.float32),
            pltpu.VMEM((top_count, count), jnp.int32),
            pltpu.VMEM((top_count, count), jnp.float32),
            pltpu.VMEM(stored_keys.shape, bf16),
            pltpu.VMEM(stored_values.shape, bf16),
            pltpu.VMEM(w_gate.shape[1:], bf16),
            pltpu.VMEM(w_up.shape[1:], bf16),
            pltpu.VMEM(w_down.shape[1:], bf16),
            pltpu.VMEM((count, width), jnp.float32),
            pltpu.VMEM((devices * count, width + LANES), bf16),
            pltpu.VMEM((4 * count, hidden_units), bf16),
            pltpu.VMEM((devices * count, width), bf16),
            pltpu.VMEM((devices * count // 2, width), bf16),
            pltpu.VMEM((line * count, width), bf16),
            pltpu.VMEM((line * count, width), bf16),
            pltpu.VMEM((line * count, width), bf16),
            pltpu.VMEM((line * count, width), bf16),
            dma((5,)),
            dma((count // GROUP, 2)),
            dma((3,)),
            dma((line, 2)),
            dma((line, 2)),
            dma((line, 2)),
            dma((line, 2)),
            dma((line, 2, 2)),
            dma((line, 2, 2)),
            dma((line,)),
            dma((line,)),
            dma((line, 2)),
            dma((line, 2)),
            dma((line, 2)),
            dma((line, 2)),
        ],
        compiler_params=pltpu.CompilerParams(
            collective_id=0, has_side_effects=True, vmem_limit_bytes=60 * 1024 * 1024
        ),
        name="gathered_layer",
    )(
        hidden_in,
        queries,
        stored_lengths,
        norm_gain[None, :],
        expert_ids.T,
        gate_weights.T,
        stored_keys,
        stored_values,
        w_gate,
        w_up,
        w_down,
    )


def gather_suits(devices, local_experts, count, top_count):
    return (
        local_experts == 1
        and devices >= 8
        and devices & (devices - 1) == 0
        and 2 * devices <= LANES
        and count % 32 == 0
        and count <= LANES
        and 2 * top_count >= devices
    )


def local(
    hidden_in,
    queries,
    stored_keys,
    stored_values,
    stored_lengths,
    norm_gain,
    expert_ids,
    gate_weights,
    w_gate,
    w_up,
    w_down,
):
    devices = lax.axis_size("ep")
    if gather_suits(devices, w_gate.shape[0], hidden_in.shape[0], expert_ids.shape[1]):
        return gathered_layer(
            hidden_in,
            queries,
            stored_keys,
            stored_values,
            stored_lengths,
            norm_gain,
            expert_ids,
            gate_weights,
            w_gate,
            w_up,
            w_down,
        )
    experts = devices * w_gate.shape[0]
    top_count = expert_ids.shape[1]
    capacity = max(2, 3 * MB_ROWS * top_count // (2 * experts))
    return layer_rows(
        hidden_in,
        queries,
        stored_keys,
        stored_values,
        stored_lengths,
        norm_gain,
        expert_ids,
        gate_weights,
        w_gate,
        w_up,
        w_down,
        MB * capacity,
    )


def solution(mesh):
    in_specs = (
        P(("groups", "ep"), None),
        P(("groups", "ep"), None),
        P(("groups", "ep"), None, None),
        P(("groups", "ep"), None, None),
        P(("groups", "ep")),
        P(),
        P(("groups", "ep"), None),
        P(("groups", "ep"), None),
        P("ep", None, None),
        P("ep", None, None),
        P("ep", None, None),
    )
    out_specs = P(("groups", "ep"), None)
    return jax.shard_map(local, mesh=mesh, in_specs=in_specs, out_specs=out_specs, check_vma=False)
```

```python
import functools
import math

import jax
import jax.numpy as jnp
from jax import lax
from jax.experimental import pallas as pl
from jax.experimental.pallas import tpu as pltpu
from jax.sharding import PartitionSpec as P

QUERY_HEADS = 16
KEY_VALUE_HEADS = 2
MB = 2
MB_ROWS = 16


def cached_attention(queries, stored_keys, stored_values, stored_lengths, heads, kv_heads):
    row_count = queries.shape[0]
    slots = stored_keys.shape[1]
    head_size = queries.shape[1] // heads
    query_head_rows = queries.reshape(row_count, kv_heads, heads // kv_heads, head_size)
    key_head_rows = stored_keys.reshape(row_count, slots, kv_heads, head_size)
    value_head_rows = stored_values.reshape(row_count, slots, kv_heads, head_size)
    scores = jnp.einsum(
        "nkgd,nckd->nkgc", query_head_rows, key_head_rows, preferred_element_type=jnp.float32
    ) / math.sqrt(head_size)
    visible = jnp.arange(slots, dtype=jnp.int32)[None, :] < stored_lengths[:, None]
    visible = visible[:, None, None, :]
    scores = jnp.where(visible, scores, -1e30)
    top_score = jnp.max(scores, axis=-1, keepdims=True)
    expo = jnp.where(visible, jnp.exp(scores - top_score), 0.0)
    probs = (expo / jnp.sum(expo, axis=-1, keepdims=True)).astype(jnp.bfloat16)
    attention_output = jnp.einsum(
        "nkgc,nckd->nkgd", probs, value_head_rows, preferred_element_type=jnp.float32
    )
    return attention_output.reshape(row_count, heads * head_size)


def expert_work(blocks, w_gate, w_up, w_down):
    gate_part = jnp.einsum("secd,edf->secf", blocks, w_gate, preferred_element_type=jnp.float32)
    up_part = jnp.einsum("secd,edf->secf", blocks, w_up, preferred_element_type=jnp.float32)
    inner = (jax.nn.silu(gate_part) * up_part).astype(jnp.bfloat16)
    return jnp.einsum("secf,efd->secd", inner, w_down, preferred_element_type=jnp.float32).astype(
        jnp.bfloat16
    )


def routed(normed, expert_ids, gate_weights, w_gate, w_up, w_down, capacity):
    devices = lax.axis_size("ep")
    local_count = w_gate.shape[0]
    experts = devices * local_count
    width = normed.shape[1]
    row_count, top_count = expert_ids.shape
    flat_ids = expert_ids.reshape(-1)
    onehot_table = (flat_ids[:, None] == jnp.arange(experts, dtype=jnp.int32)[None, :]).astype(
        jnp.int32
    )
    before = jnp.cumsum(onehot_table, axis=0) - onehot_table
    slot_index = jnp.sum(before * onehot_table, axis=1)
    target = flat_ids * capacity + slot_index
    target_rows = target.reshape(row_count, top_count)
    placing = jnp.sum(
        (
            target_rows[:, :, None]
            == jnp.arange(experts * capacity, dtype=jnp.int32)[None, None, :]
        ).astype(jnp.float32),
        axis=1,
    ).astype(jnp.bfloat16)
    buffer = jnp.einsum("tp,td->pd", placing, normed, preferred_element_type=jnp.float32).astype(
        jnp.bfloat16
    )
    buffer = buffer.reshape(experts, capacity, width)
    arrived = lax.all_to_all(buffer, "ep", split_axis=0, concat_axis=0, tiled=True)
    item_count = arrived.shape[1]
    blocks = arrived.reshape(devices, local_count, item_count, width)
    finished = expert_work(blocks, w_gate, w_up, w_down).reshape(experts, item_count, width)
    results = lax.all_to_all(finished, "ep", split_axis=0, concat_axis=0, tiled=True)
    picked = jnp.take(results.reshape(experts * capacity, width), target, axis=0)
    picked = picked.reshape(row_count, top_count, width).astype(jnp.float32)
    return jnp.sum(picked * gate_weights[:, :, None], axis=1)


def layer_rows(
    hidden_in,
    queries,
    stored_keys,
    stored_values,
    stored_lengths,
    norm_gain,
    expert_ids,
    gate_weights,
    w_gate,
    w_up,
    w_down,
    capacity,
):
    attention_output = cached_attention(
        queries, stored_keys, stored_values, stored_lengths, QUERY_HEADS, KEY_VALUE_HEADS
    )
    resid = hidden_in.astype(jnp.float32) + attention_output
    mean_square = jnp.mean(resid * resid, axis=-1, keepdims=True)
    normed = (resid * lax.rsqrt(mean_square + 1e-06) * norm_gain[None, :]).astype(jnp.bfloat16)
    mixture = routed(normed, expert_ids, gate_weights, w_gate, w_up, w_down, capacity)
    return (resid + mixture).astype(jnp.bfloat16)


LANES = 128
GROUP = 8


def chip_at(position, chips):
    half = chips // 2
    return jnp.where(position < half, 2 * position, 2 * (chips - 1 - position) + 1)


def position_of(chip, chips):
    return jnp.where(lax.rem(chip, 2) == 0, chip // 2, chips - 1 - chip // 2)


def tile_of(extent, most):
    return max(t for t in range(LANES, most + 1, LANES) if extent % t == 0)


def layer_kernel(
    devices,
    heads,
    kv_heads,
    hidden_hbm,
    queries_hbm,
    lengths_ref,
    gain_hbm,
    ids_hbm,
    weights_hbm,
    keys_hbm,
    values_hbm,
    gate_hbm,
    up_hbm,
    down_hbm,
    out_ref,
    hidden_ref,
    queries_ref,
    gain_ref,
    ids_ref,
    weights_ref,
    keys_ref,
    values_ref,
    gate_ref,
    up_ref,
    down_ref,
    resid_ref,
    rows_ref,
    inner_ref,
    own_ref,
    sibling_ref,
    outgoing_ref,
    incoming_ref,
    small_sem,
    kv_sem,
    w_sem,
    ring_send,
    ring_recv,
    pair_send,
    pair_recv,
    back_pair_send,
    back_pair_recv,
    back_send,
    back_recv,
):
    chips = devices // 2
    hops = chips // 2
    count, width = hidden_ref.shape
    slots = keys_ref.shape[1]
    head_size = width // heads
    per_kv = heads // kv_heads
    half = count // 2
    top_count = ids_ref.shape[0]
    hidden_units = gate_ref.shape[1]

    me = lax.axis_index("ep")
    core = lax.rem(me, 2)
    position = position_of(me // 2, chips)
    right = chip_at(lax.rem(position + 1, chips), chips) * 2 + core
    left = chip_at(lax.rem(position + chips - 1, chips), chips) * 2 + core
    sibling = me + 1 - 2 * core
    onward = (right, left)

    small_copies = []
    for j, (src, dst) in enumerate(
        (
            (queries_hbm, queries_ref),
            (hidden_hbm, hidden_ref),
            (gain_hbm, gain_ref),
            (ids_hbm, ids_ref),
            (weights_hbm, weights_ref),
        )
    ):
        copy = pltpu.make_async_copy(src, dst, small_sem.at[j])
        copy.start()
        small_copies.append(copy)
    groups = count // GROUP
    kv_copies = []
    for i in range(groups):
        part = pl.ds(i * GROUP, GROUP)
        for j, (src, dst) in enumerate(((keys_hbm, keys_ref), (values_hbm, values_ref))):
            copy = pltpu.make_async_copy(src.at[part], dst.at[part], kv_sem.at[i, j])
            copy.start()
            kv_copies.append(copy)
    barrier = pltpu.get_barrier_semaphore()
    others = [left, right, sibling]
    for other in others:
        pl.semaphore_signal(
            barrier, inc=1, device_id={"ep": other}, device_id_type=pl.DeviceIdType.MESH
        )
    for copy in small_copies:
        copy.wait()

    scale = 1.0 / math.sqrt(head_size)
    square_rows = per_kv * GROUP
    row_id = lax.broadcasted_iota(jnp.int32, (square_rows, GROUP * slots), 0)
    col_id = lax.broadcasted_iota(jnp.int32, (square_rows, GROUP * slots), 1)
    column_request = col_id // slots
    same_request = (row_id % GROUP) == column_request
    slot_id = col_id % slots
    def attend(i):
        kv_copies[2 * i].wait()
        kv_copies[2 * i + 1].wait()
        part = pl.ds(i * GROUP, GROUP)
        lengths = jnp.zeros((square_rows, GROUP * slots), jnp.int32)
        for r in range(GROUP):
            lengths = jnp.where(column_request == r, lengths_ref[i * GROUP + r], lengths)
        visible = same_request & (slot_id < lengths)
        group_queries = queries_ref[part, :].astype(jnp.float32)
        hidden = hidden_ref[part, :].astype(jnp.float32)
        for g in range(kv_heads):
            lanes = slice(g * head_size, (g + 1) * head_size)
            first = g * per_kv
            q = jnp.concatenate(
                [
                    group_queries[:, (first + h) * head_size : (first + h + 1) * head_size]
                    for h in range(per_kv)
                ],
                axis=0,
            ).astype(jnp.bfloat16)
            k = keys_ref[part, :, lanes].reshape(GROUP * slots, head_size)
            v = values_ref[part, :, lanes].reshape(GROUP * slots, head_size)
            scores = (
                lax.dot_general(q, k, (((1,), (1,)), ((), ())), preferred_element_type=jnp.float32)
                * scale
            )
            scores = jnp.where(visible, scores, -1e30)
            expo = jnp.where(visible, jnp.exp(scores - jnp.max(scores, axis=-1, keepdims=True)), 0.0)
            probs = (expo / jnp.sum(expo, axis=-1, keepdims=True)).astype(jnp.bfloat16)
            attended = jnp.dot(probs, v, preferred_element_type=jnp.float32)
            for h in range(per_kv):
                cols = slice((first + h) * head_size, (first + h + 1) * head_size)
                resid_ref[part, cols] = hidden[:, cols] + attended[h * GROUP : (h + 1) * GROUP, :]

    spare = LANES - count
    ids = jnp.concatenate([ids_ref[...], jnp.zeros((top_count, spare), jnp.int32)], axis=1)
    weights = jnp.concatenate([weights_ref[...], jnp.zeros((top_count, spare), jnp.float32)], axis=1)
    expert_id = lax.broadcasted_iota(jnp.int32, (LANES, LANES), 0)
    turned = jnp.zeros((LANES, LANES), jnp.float32)
    for k in range(top_count):
        chosen = ids[k : k + 1, :]
        turned = turned + jnp.where(
            (expert_id == chosen) | (expert_id == chosen + devices), weights[k : k + 1, :], 0.0
        )
    table = turned.T[0:count, :]
    lane = lax.broadcasted_iota(jnp.int32, (count, LANES), 1)
    coarse = table.astype(jnp.bfloat16)
    fine = (table - coarse.astype(jnp.float32)).astype(jnp.bfloat16)
    rows_ref[0:count, width : width + LANES] = jnp.where(
        lane < devices, coarse.astype(jnp.float32), fine.astype(jnp.float32)
    ).astype(jnp.bfloat16)

    def normalize(h):
        part = pl.ds(h * half, half)
        resid = resid_ref[part, :]
        mean_square = jnp.mean(resid * resid, axis=-1, keepdims=True)
        rows_ref[part, 0:width] = (
            resid * lax.rsqrt(mean_square + 1e-06) * gain_ref[...]
        ).astype(jnp.bfloat16)

    def chunk(s):
        return 0 if s == 0 else 2 * count + (s - 1) * 4 * count

    def own_rows(s):
        return 0 if s == 0 else count + (s - 1) * 2 * count

    def half_at(s, direction, h):
        if s in (0, hops):
            return chunk(s) + h * half
        return chunk(s) + direction * count + h * half

    def remote(src, dst, send, recv, other):
        return pltpu.make_async_remote_copy(
            src_ref=src,
            dst_ref=dst,
            send_sem=send,
            recv_sem=recv,
            device_id={"ep": other},
            device_id_type=pl.DeviceIdType.MESH,
        )

    def travels(s, direction, h):
        return s < hops or h == direction

    def ring_copy(s, direction, h):
        source = half_at(s - 1, direction, h)
        return remote(
            rows_ref.at[pl.ds(source, half)],
            rows_ref.at[pl.ds(half_at(s, direction, h), half)],
            ring_send.at[s - 1, direction, h],
            ring_recv.at[s - 1, direction, h],
            onward[direction],
        )

    def pair_copy(s, direction, h):
        start = half_at(s, direction, h)
        size = count if s in (0, hops) else 2 * count
        return remote(
            rows_ref.at[pl.ds(start, half)],
            rows_ref.at[pl.ds(start + size, half)],
            pair_send.at[s, direction, h],
            pair_recv.at[s, direction, h],
            sibling,
        )

    sent = []

    def go(copy):
        copy.start()
        sent.append(copy)

    def home(h):
        return pair_copy(0, 0, h)

    w_copies = []
    for h in range(2):
        for i in range(h * groups // 2, (h + 1) * groups // 2):
            attend(i)
        normalize(h)
        if h == 0:
            pl.semaphore_wait(barrier, len(others))
        for direction in range(2):
            go(ring_copy(1, direction, h))
        go(home(h))
        if h == 0:
            for j, (src, dst) in enumerate(((gate_hbm, gate_ref), (up_hbm, up_ref), (down_hbm, down_ref))):
                copy = pltpu.make_async_copy(src.at[0], dst, w_sem.at[j])
                copy.start()
                w_copies.append(copy)

    f_tile = tile_of(hidden_units, 256)
    d_tile = tile_of(width, 512)

    def expert(start, size):
        span = pl.ds(start, size)

        def first(i):
            cols = slice(i * f_tile, (i + 1) * f_tile)
            x = rows_ref[span, 0:width]
            gate = jnp.dot(x, gate_ref[:, cols], preferred_element_type=jnp.float32)
            up = jnp.dot(x, up_ref[:, cols], preferred_element_type=jnp.float32)
            inner_ref[0:size, cols] = (gate / (1.0 + jnp.exp(-gate)) * up).astype(jnp.bfloat16)

        def second(i):
            cols = slice(i * d_tile, (i + 1) * d_tile)
            spot = lax.broadcasted_iota(jnp.int32, (size, LANES), 1)
            both = rows_ref[span, width : width + LANES].astype(jnp.float32)
            weight = jnp.sum(
                jnp.where((spot == me) | (spot == me + devices), both, 0.0), axis=-1, keepdims=True
            )
            result = jnp.dot(
                inner_ref[0:size, :], down_ref[:, cols], preferred_element_type=jnp.float32
            )
            own_ref[span, cols] = (result * weight).astype(jnp.bfloat16)

        steps = [functools.partial(first, i) for i in range(hidden_units // f_tile)]
        return steps + [functools.partial(second, i) for i in range(width // d_tile)]

    def back_pair(s):
        size = count if s in (0, hops) else 2 * count
        return remote(
            own_ref.at[pl.ds(chunk(s) + size, size)],
            sibling_ref.at[pl.ds(own_rows(s), size)],
            back_pair_send.at[s],
            back_pair_recv.at[s],
            sibling,
        )

    pending = []

    def run(amount):
        for _ in range(min(amount, len(pending))):
            pending.pop(0)()

    def after(s):
        if s == 1:
            for copy in w_copies:
                copy.wait()
            for h in range(2):
                home(h).wait_recv()
        for h in range(2):
            for direction in range(2):
                if travels(s, direction, h):
                    pair_copy(s, direction, h).wait_recv()
        if s == hops - 1 and s > 1:
            return
        first = 0 if s == 1 else s - 1 if s == hops else s
        pending.extend(expert(chunk(first), chunk(s) - chunk(first) + (2 if s == hops else 4) * count))
        for i in range(first, s + 1):
            pending.append(lambda i=i: go(back_pair(i)))

    for s in range(1, hops + 1):
        for h in range(2):
            for direction in range(2):
                if travels(s, direction, h):
                    ring_copy(s, direction, h).wait_recv()
                    if s < hops and travels(s + 1, direction, h):
                        go(ring_copy(s + 1, direction, h))
                    go(pair_copy(s, direction, h))
            run(3)
        run(len(pending) - 3 if s < hops else len(pending))
        after(s)
        run(2 if s < hops else len(pending))

    def back_copy(s, direction, h):
        return remote(
            outgoing_ref.at[direction, s - 1, pl.ds(h * half, half)],
            incoming_ref.at[direction, s - 1, pl.ds(h * half, half)],
            back_send.at[s - 1, direction, h],
            back_recv.at[s - 1, direction, h],
            onward[1 - direction],
        )

    def pass_back(s, direction, h):
        start = half_at(s, direction, h)
        offset = start - chunk(s) + own_rows(s)
        total = own_ref[pl.ds(start, half), :].astype(jnp.float32) + sibling_ref[
            pl.ds(offset, half), :
        ].astype(jnp.float32)
        if s < hops and travels(s + 1, direction, h):
            back_copy(s + 1, direction, h).wait_recv()
            total = total + incoming_ref[direction, s, pl.ds(h * half, half), :].astype(jnp.float32)
        outgoing_ref[direction, s - 1, pl.ds(h * half, half), :] = total.astype(jnp.bfloat16)
        go(back_copy(s, direction, h))

    for s in range(hops, 0, -1):
        if s == hops:
            back_pair(s).wait_recv()
        for direction in range(2):
            pass_back(s, direction, direction)
        if s > 1:
            back_pair(s - 1).wait_recv()
            for direction in range(2):
                pass_back(s - 1, direction, 1 - direction)

    back_pair(0).wait_recv()
    for h in range(2):
        span = pl.ds(h * half, half)
        total = own_ref[span, :].astype(jnp.float32) + sibling_ref[span, :].astype(jnp.float32)
        total = total + resid_ref[span, :]
        for direction in range(2):
            back_copy(1, direction, h).wait_recv()
            total = total + incoming_ref[direction, 0, span, :].astype(jnp.float32)
        out_ref[span, :] = total.astype(jnp.bfloat16)

    for copy in sent:
        copy.wait_send()


def gathered_layer(
    hidden_in,
    queries,
    stored_keys,
    stored_values,
    stored_lengths,
    norm_gain,
    expert_ids,
    gate_weights,
    w_gate,
    w_up,
    w_down,
):
    devices = lax.axis_size("ep")
    count, width = hidden_in.shape
    hidden_units = w_gate.shape[2]
    hops = devices // 4
    vmem = pl.BlockSpec(memory_space=pltpu.VMEM)
    smem = pl.BlockSpec(memory_space=pltpu.SMEM)
    hbm = pl.BlockSpec(memory_space=pltpu.HBM)
    dma = pltpu.SemaphoreType.DMA
    bf16 = jnp.bfloat16
    top_count = expert_ids.shape[1]
    return pl.pallas_call(
        functools.partial(layer_kernel, devices, QUERY_HEADS, KEY_VALUE_HEADS),
        out_shape=jax.ShapeDtypeStruct((count, width), bf16),
        in_specs=[hbm, hbm, smem] + [hbm] * 8,
        out_specs=vmem,
        scratch_shapes=[
            pltpu.VMEM((count, width), bf16),
            pltpu.VMEM((count, width), bf16),
            pltpu.VMEM((1, width), jnp.float32),
            pltpu.VMEM((top_count, count), jnp.int32),
            pltpu.VMEM((top_count, count), jnp.float32),
            pltpu.VMEM(stored_keys.shape, bf16),
            pltpu.VMEM(stored_values.shape, bf16),
            pltpu.VMEM(w_gate.shape[1:], bf16),
            pltpu.VMEM(w_up.shape[1:], bf16),
            pltpu.VMEM(w_down.shape[1:], bf16),
            pltpu.VMEM((count, width), jnp.float32),
            pltpu.VMEM((devices * count, width + LANES), bf16),
            pltpu.VMEM((6 * count, hidden_units), bf16),
            pltpu.VMEM((devices * count, width), bf16),
            pltpu.VMEM((devices * count // 2, width), bf16),
            pltpu.VMEM((2, hops, count, width), bf16),
            pltpu.VMEM((2, hops, count, width), bf16),
            dma((5,)),
            dma((count // GROUP, 2)),
            dma((3,)),
            dma((hops, 2, 2)),
            dma((hops, 2, 2)),
            dma((hops + 1, 2, 2)),
            dma((hops + 1, 2, 2)),
            dma((hops + 1,)),
            dma((hops + 1,)),
            dma((hops, 2, 2)),
            dma((hops, 2, 2)),
        ],
        compiler_params=pltpu.CompilerParams(
            collective_id=0, has_side_effects=True, vmem_limit_bytes=60 * 1024 * 1024
        ),
        name="gathered_layer",
    )(
        hidden_in,
        queries,
        stored_lengths,
        norm_gain[None, :],
        expert_ids.T,
        gate_weights.T,
        stored_keys,
        stored_values,
        w_gate,
        w_up,
        w_down,
    )


def gather_suits(devices, local_experts, count, top_count):
    return (
        local_experts == 1
        and devices % 8 == 0
        and 2 * devices <= LANES
        and count % 32 == 0
        and count <= LANES
        and 2 * top_count >= devices
    )


def local(
    hidden_in,
    queries,
    stored_keys,
    stored_values,
    stored_lengths,
    norm_gain,
    expert_ids,
    gate_weights,
    w_gate,
    w_up,
    w_down,
):
    devices = lax.axis_size("ep")
    if gather_suits(devices, w_gate.shape[0], hidden_in.shape[0], expert_ids.shape[1]):
        return gathered_layer(
            hidden_in,
            queries,
            stored_keys,
            stored_values,
            stored_lengths,
            norm_gain,
            expert_ids,
            gate_weights,
            w_gate,
            w_up,
            w_down,
        )
    experts = devices * w_gate.shape[0]
    top_count = expert_ids.shape[1]
    capacity = max(2, 3 * MB_ROWS * top_count // (2 * experts))
    return layer_rows(
        hidden_in,
        queries,
        stored_keys,
        stored_values,
        stored_lengths,
        norm_gain,
        expert_ids,
        gate_weights,
        w_gate,
        w_up,
        w_down,
        MB * capacity,
    )


def solution(mesh):
    in_specs = (
        P(("groups", "ep"), None),
        P(("groups", "ep"), None),
        P(("groups", "ep"), None, None),
        P(("groups", "ep"), None, None),
        P(("groups", "ep")),
        P(),
        P(("groups", "ep"), None),
        P(("groups", "ep"), None),
        P("ep", None, None),
        P("ep", None, None),
        P("ep", None, None),
    )
    out_specs = P(("groups", "ep"), None)
    return jax.shard_map(local, mesh=mesh, in_specs=in_specs, out_specs=out_specs, check_vma=False)
```

```python
import functools
import math

import jax
import jax.numpy as jnp
from jax import lax
from jax.experimental import pallas as pl
from jax.experimental.pallas import tpu as pltpu
from jax.sharding import PartitionSpec as P

QUERY_HEADS = 16
KEY_VALUE_HEADS = 2
MB = 2
MB_ROWS = 16


def cached_attention(queries, stored_keys, stored_values, stored_lengths, heads, kv_heads):
    row_count = queries.shape[0]
    slots = stored_keys.shape[1]
    head_size = queries.shape[1] // heads
    query_head_rows = queries.reshape(row_count, kv_heads, heads // kv_heads, head_size)
    key_head_rows = stored_keys.reshape(row_count, slots, kv_heads, head_size)
    value_head_rows = stored_values.reshape(row_count, slots, kv_heads, head_size)
    scores = jnp.einsum(
        "nkgd,nckd->nkgc", query_head_rows, key_head_rows, preferred_element_type=jnp.float32
    ) / math.sqrt(head_size)
    visible = jnp.arange(slots, dtype=jnp.int32)[None, :] < stored_lengths[:, None]
    visible = visible[:, None, None, :]
    scores = jnp.where(visible, scores, -1e30)
    top_score = jnp.max(scores, axis=-1, keepdims=True)
    expo = jnp.where(visible, jnp.exp(scores - top_score), 0.0)
    probs = (expo / jnp.sum(expo, axis=-1, keepdims=True)).astype(jnp.bfloat16)
    attention_output = jnp.einsum(
        "nkgc,nckd->nkgd", probs, value_head_rows, preferred_element_type=jnp.float32
    )
    return attention_output.reshape(row_count, heads * head_size)


def expert_work(blocks, w_gate, w_up, w_down):
    gate_part = jnp.einsum("secd,edf->secf", blocks, w_gate, preferred_element_type=jnp.float32)
    up_part = jnp.einsum("secd,edf->secf", blocks, w_up, preferred_element_type=jnp.float32)
    inner = (jax.nn.silu(gate_part) * up_part).astype(jnp.bfloat16)
    return jnp.einsum("secf,efd->secd", inner, w_down, preferred_element_type=jnp.float32).astype(
        jnp.bfloat16
    )


def routed(normed, expert_ids, gate_weights, w_gate, w_up, w_down, capacity):
    devices = lax.axis_size("ep")
    local_count = w_gate.shape[0]
    experts = devices * local_count
    width = normed.shape[1]
    row_count, top_count = expert_ids.shape
    flat_ids = expert_ids.reshape(-1)
    onehot_table = (flat_ids[:, None] == jnp.arange(experts, dtype=jnp.int32)[None, :]).astype(
        jnp.int32
    )
    before = jnp.cumsum(onehot_table, axis=0) - onehot_table
    slot_index = jnp.sum(before * onehot_table, axis=1)
    target = flat_ids * capacity + slot_index
    target_rows = target.reshape(row_count, top_count)
    placing = jnp.sum(
        (
            target_rows[:, :, None]
            == jnp.arange(experts * capacity, dtype=jnp.int32)[None, None, :]
        ).astype(jnp.float32),
        axis=1,
    ).astype(jnp.bfloat16)
    buffer = jnp.einsum("tp,td->pd", placing, normed, preferred_element_type=jnp.float32).astype(
        jnp.bfloat16
    )
    buffer = buffer.reshape(experts, capacity, width)
    arrived = lax.all_to_all(buffer, "ep", split_axis=0, concat_axis=0, tiled=True)
    item_count = arrived.shape[1]
    blocks = arrived.reshape(devices, local_count, item_count, width)
    finished = expert_work(blocks, w_gate, w_up, w_down).reshape(experts, item_count, width)
    results = lax.all_to_all(finished, "ep", split_axis=0, concat_axis=0, tiled=True)
    picked = jnp.take(results.reshape(experts * capacity, width), target, axis=0)
    picked = picked.reshape(row_count, top_count, width).astype(jnp.float32)
    return jnp.sum(picked * gate_weights[:, :, None], axis=1)


def layer_rows(
    hidden_in,
    queries,
    stored_keys,
    stored_values,
    stored_lengths,
    norm_gain,
    expert_ids,
    gate_weights,
    w_gate,
    w_up,
    w_down,
    capacity,
):
    attention_output = cached_attention(
        queries, stored_keys, stored_values, stored_lengths, QUERY_HEADS, KEY_VALUE_HEADS
    )
    resid = hidden_in.astype(jnp.float32) + attention_output
    mean_square = jnp.mean(resid * resid, axis=-1, keepdims=True)
    normed = (resid * lax.rsqrt(mean_square + 1e-06) * norm_gain[None, :]).astype(jnp.bfloat16)
    mixture = routed(normed, expert_ids, gate_weights, w_gate, w_up, w_down, capacity)
    return (resid + mixture).astype(jnp.bfloat16)


LANES = 128
GROUP = 8


def chip_at(position, chips):
    half = chips // 2
    return jnp.where(position < half, 2 * position, 2 * (chips - 1 - position) + 1)


def position_of(chip, chips):
    return jnp.where(lax.rem(chip, 2) == 0, chip // 2, chips - 1 - chip // 2)


def tile_of(extent, most):
    return max(t for t in range(LANES, most + 1, LANES) if extent % t == 0)


def layer_kernel(
    devices,
    heads,
    kv_heads,
    hidden_hbm,
    queries_hbm,
    lengths_ref,
    gain_hbm,
    ids_hbm,
    weights_hbm,
    keys_hbm,
    values_hbm,
    gate_hbm,
    up_hbm,
    down_hbm,
    out_ref,
    hidden_ref,
    queries_ref,
    gain_ref,
    ids_ref,
    weights_ref,
    keys_ref,
    values_ref,
    gate_ref,
    up_ref,
    down_ref,
    resid_ref,
    rows_ref,
    inner_ref,
    own_ref,
    sibling_ref,
    outgoing_ref,
    incoming_ref,
    small_sem,
    kv_sem,
    w_sem,
    ring_send,
    ring_recv,
    pair_send,
    pair_recv,
    back_pair_send,
    back_pair_recv,
    back_send,
    back_recv,
):
    chips = devices // 2
    hops = chips // 2
    count, width = hidden_ref.shape
    slots = keys_ref.shape[1]
    head_size = width // heads
    per_kv = heads // kv_heads
    half = count // 2
    top_count = ids_ref.shape[0]
    hidden_units = gate_ref.shape[1]

    me = lax.axis_index("ep")
    core = lax.rem(me, 2)
    position = position_of(me // 2, chips)
    right = chip_at(lax.rem(position + 1, chips), chips) * 2 + core
    left = chip_at(lax.rem(position + chips - 1, chips), chips) * 2 + core
    sibling = me + 1 - 2 * core
    onward = (right, left)

    small_copies = []
    for j, (src, dst) in enumerate(
        (
            (queries_hbm, queries_ref),
            (hidden_hbm, hidden_ref),
            (gain_hbm, gain_ref),
            (ids_hbm, ids_ref),
            (weights_hbm, weights_ref),
        )
    ):
        copy = pltpu.make_async_copy(src, dst, small_sem.at[j])
        copy.start()
        small_copies.append(copy)
    groups = count // GROUP
    kv_copies = []
    for i in range(groups):
        part = pl.ds(i * GROUP, GROUP)
        for j, (src, dst) in enumerate(((keys_hbm, keys_ref), (values_hbm, values_ref))):
            copy = pltpu.make_async_copy(src.at[part], dst.at[part], kv_sem.at[i, j])
            copy.start()
            kv_copies.append(copy)
    barrier = pltpu.get_barrier_semaphore()
    others = [left, right, sibling]
    for other in others:
        pl.semaphore_signal(
            barrier, inc=1, device_id={"ep": other}, device_id_type=pl.DeviceIdType.MESH
        )
    for copy in small_copies:
        copy.wait()

    scale = 1.0 / math.sqrt(head_size)
    square_rows = per_kv * GROUP
    row_id = lax.broadcasted_iota(jnp.int32, (square_rows, GROUP * slots), 0)
    col_id = lax.broadcasted_iota(jnp.int32, (square_rows, GROUP * slots), 1)
    column_request = col_id // slots
    same_request = (row_id % GROUP) == column_request
    slot_id = col_id % slots
    def attend(i):
        part = pl.ds(i * GROUP, GROUP)
        lengths = jnp.zeros((square_rows, GROUP * slots), jnp.int32)
        for r in range(GROUP):
            lengths = jnp.where(column_request == r, lengths_ref[i * GROUP + r], lengths)
        visible = same_request & (slot_id < lengths)
        group_queries = queries_ref[part, :].astype(jnp.float32)
        hidden = hidden_ref[part, :].astype(jnp.float32)
        for g in range(kv_heads):
            lanes = slice(g * head_size, (g + 1) * head_size)
            first = g * per_kv
            q = jnp.concatenate(
                [
                    group_queries[:, (first + h) * head_size : (first + h + 1) * head_size]
                    for h in range(per_kv)
                ],
                axis=0,
            ).astype(jnp.bfloat16)
            k = keys_ref[part, :, lanes].reshape(GROUP * slots, head_size)
            v = values_ref[part, :, lanes].reshape(GROUP * slots, head_size)
            scores = (
                lax.dot_general(q, k, (((1,), (1,)), ((), ())), preferred_element_type=jnp.float32)
                * scale
            )
            scores = jnp.where(visible, scores, -1e30)
            expo = jnp.exp(scores - jnp.max(scores, axis=-1, keepdims=True))
            probs = (expo * (1.0 / jnp.sum(expo, axis=-1, keepdims=True))).astype(jnp.bfloat16)
            attended = jnp.dot(probs, v, preferred_element_type=jnp.float32)
            for h in range(per_kv):
                cols = slice((first + h) * head_size, (first + h + 1) * head_size)
                resid_ref[part, cols] = hidden[:, cols] + attended[h * GROUP : (h + 1) * GROUP, :]

    spare = LANES - count
    ids = jnp.concatenate([ids_ref[...], jnp.zeros((top_count, spare), jnp.int32)], axis=1)
    weights = jnp.concatenate([weights_ref[...], jnp.zeros((top_count, spare), jnp.float32)], axis=1)
    expert_id = lax.broadcasted_iota(jnp.int32, (LANES, LANES), 0)
    turned = jnp.zeros((LANES, LANES), jnp.float32)
    for k in range(top_count):
        chosen = ids[k : k + 1, :]
        turned = turned + jnp.where(
            (expert_id == chosen) | (expert_id == chosen + devices), weights[k : k + 1, :], 0.0
        )
    table = turned.T[0:count, :]
    lane = lax.broadcasted_iota(jnp.int32, (count, LANES), 1)
    coarse = table.astype(jnp.bfloat16)
    fine = (table - coarse.astype(jnp.float32)).astype(jnp.bfloat16)
    rows_ref[0:count, width : width + LANES] = jnp.where(
        lane < devices, coarse.astype(jnp.float32), fine.astype(jnp.float32)
    ).astype(jnp.bfloat16)

    def normalize(h):
        part = pl.ds(h * half, half)
        resid = resid_ref[part, :]
        mean_square = jnp.mean(resid * resid, axis=-1, keepdims=True)
        rows_ref[part, 0:width] = (
            resid * lax.rsqrt(mean_square + 1e-06) * gain_ref[...]
        ).astype(jnp.bfloat16)

    def chunk(s):
        return 0 if s == 0 else 2 * count + (s - 1) * 4 * count

    def own_rows(s):
        return 0 if s == 0 else count + (s - 1) * 2 * count

    def half_at(s, direction, h):
        if s in (0, hops):
            return chunk(s) + h * half
        return chunk(s) + direction * count + h * half

    def remote(src, dst, send, recv, other):
        return pltpu.make_async_remote_copy(
            src_ref=src,
            dst_ref=dst,
            send_sem=send,
            recv_sem=recv,
            device_id={"ep": other},
            device_id_type=pl.DeviceIdType.MESH,
        )

    def travels(s, direction, h):
        return s < hops or h == direction

    def ring_copy(s, direction, h):
        source = half_at(s - 1, direction, h)
        return remote(
            rows_ref.at[pl.ds(source, half)],
            rows_ref.at[pl.ds(half_at(s, direction, h), half)],
            ring_send.at[s - 1, direction, h],
            ring_recv.at[s - 1, direction, h],
            onward[direction],
        )

    def pair_copy(s, direction, h):
        start = half_at(s, direction, h)
        size = count if s in (0, hops) else 2 * count
        return remote(
            rows_ref.at[pl.ds(start, half)],
            rows_ref.at[pl.ds(start + size, half)],
            pair_send.at[s, direction, h],
            pair_recv.at[s, direction, h],
            sibling,
        )

    sent = []

    def go(copy):
        copy.start()
        sent.append(copy)

    def home(h):
        return pair_copy(0, 0, h)

    w_copies = []
    for h in range(2):
        for copy in kv_copies[h * groups : (h + 1) * groups]:
            copy.wait()
        for i in range(h * groups // 2, (h + 1) * groups // 2):
            attend(i)
        normalize(h)
        if h == 0:
            pl.semaphore_wait(barrier, len(others))
        for direction in range(2):
            go(ring_copy(1, direction, h))
        go(home(h))
        if h == 0:
            for j, (src, dst) in enumerate(((gate_hbm, gate_ref), (up_hbm, up_ref), (down_hbm, down_ref))):
                copy = pltpu.make_async_copy(src.at[0], dst, w_sem.at[j])
                copy.start()
                w_copies.append(copy)

    f_tile = tile_of(hidden_units, 256)
    d_tile = tile_of(width, 512)

    def expert(start, size):
        span = pl.ds(start, size)

        def first(i):
            cols = slice(i * f_tile, (i + 1) * f_tile)
            x = rows_ref[span, 0:width]
            gate = jnp.dot(x, gate_ref[:, cols], preferred_element_type=jnp.float32)
            up = jnp.dot(x, up_ref[:, cols], preferred_element_type=jnp.float32)
            inner_ref[0:size, cols] = (gate / (1.0 + jnp.exp(-gate)) * up).astype(jnp.bfloat16)

        def second(i):
            cols = slice(i * d_tile, (i + 1) * d_tile)
            spot = lax.broadcasted_iota(jnp.int32, (size, LANES), 1)
            both = rows_ref[span, width : width + LANES].astype(jnp.float32)
            weight = jnp.sum(
                jnp.where((spot == me) | (spot == me + devices), both, 0.0), axis=-1, keepdims=True
            )
            result = jnp.dot(
                inner_ref[0:size, :], down_ref[:, cols], preferred_element_type=jnp.float32
            )
            own_ref[span, cols] = (result * weight).astype(jnp.bfloat16)

        steps = [functools.partial(first, i) for i in range(hidden_units // f_tile)]
        return steps + [functools.partial(second, i) for i in range(width // d_tile)]

    def back_pair(s):
        size = count if s in (0, hops) else 2 * count
        return remote(
            own_ref.at[pl.ds(chunk(s) + size, size)],
            sibling_ref.at[pl.ds(own_rows(s), size)],
            back_pair_send.at[s],
            back_pair_recv.at[s],
            sibling,
        )

    pending = []

    def run(amount):
        for _ in range(min(amount, len(pending))):
            pending.pop(0)()

    def after(s):
        if s == 1:
            for copy in w_copies:
                copy.wait()
            for h in range(2):
                home(h).wait_recv()
        for h in range(2):
            for direction in range(2):
                if travels(s, direction, h):
                    pair_copy(s, direction, h).wait_recv()
        first = 0 if s == 1 else s
        pending.extend(expert(chunk(first), chunk(s) - chunk(first) + (2 if s == hops else 4) * count))
        for i in range(first, s + 1):
            pending.append(lambda i=i: go(back_pair(i)))

    for s in range(1, hops + 1):
        for h in range(2):
            for direction in range(2):
                if travels(s, direction, h):
                    ring_copy(s, direction, h).wait_recv()
                    if s < hops and travels(s + 1, direction, h):
                        go(ring_copy(s + 1, direction, h))
                    go(pair_copy(s, direction, h))
            run(3)
        run(len(pending))
        after(s)
        run(2 if s < hops - 1 else len(pending))

    def back_copy(s, direction, h):
        return remote(
            outgoing_ref.at[direction, s - 1, pl.ds(h * half, half)],
            incoming_ref.at[direction, s - 1, pl.ds(h * half, half)],
            back_send.at[s - 1, direction, h],
            back_recv.at[s - 1, direction, h],
            onward[1 - direction],
        )

    def pass_back(s, direction, h):
        start = half_at(s, direction, h)
        offset = start - chunk(s) + own_rows(s)
        total = own_ref[pl.ds(start, half), :].astype(jnp.float32) + sibling_ref[
            pl.ds(offset, half), :
        ].astype(jnp.float32)
        if s < hops and travels(s + 1, direction, h):
            back_copy(s + 1, direction, h).wait_recv()
            total = total + incoming_ref[direction, s, pl.ds(h * half, half), :].astype(jnp.float32)
        outgoing_ref[direction, s - 1, pl.ds(h * half, half), :] = total.astype(jnp.bfloat16)
        go(back_copy(s, direction, h))

    for s in range(hops, 0, -1):
        if s == hops:
            back_pair(s).wait_recv()
        for direction in range(2):
            pass_back(s, direction, direction)
        if s > 1:
            back_pair(s - 1).wait_recv()
            for direction in range(2):
                pass_back(s - 1, direction, 1 - direction)

    back_pair(0).wait_recv()
    for h in range(2):
        span = pl.ds(h * half, half)
        total = own_ref[span, :].astype(jnp.float32) + sibling_ref[span, :].astype(jnp.float32)
        total = total + resid_ref[span, :]
        for direction in range(2):
            back_copy(1, direction, h).wait_recv()
            total = total + incoming_ref[direction, 0, span, :].astype(jnp.float32)
        out_ref[span, :] = total

    for copy in sent:
        copy.wait_send()


def gathered_layer(
    hidden_in,
    queries,
    stored_keys,
    stored_values,
    stored_lengths,
    norm_gain,
    expert_ids,
    gate_weights,
    w_gate,
    w_up,
    w_down,
):
    devices = lax.axis_size("ep")
    count, width = hidden_in.shape
    hidden_units = w_gate.shape[2]
    hops = devices // 4
    vmem = pl.BlockSpec(memory_space=pltpu.VMEM)
    smem = pl.BlockSpec(memory_space=pltpu.SMEM)
    hbm = pl.BlockSpec(memory_space=pltpu.HBM)
    dma = pltpu.SemaphoreType.DMA
    bf16 = jnp.bfloat16
    top_count = expert_ids.shape[1]
    return pl.pallas_call(
        functools.partial(layer_kernel, devices, QUERY_HEADS, KEY_VALUE_HEADS),
        out_shape=jax.ShapeDtypeStruct((count, width), jnp.float32),
        in_specs=[hbm, hbm, smem] + [hbm] * 8,
        out_specs=vmem,
        scratch_shapes=[
            pltpu.VMEM((count, width), bf16),
            pltpu.VMEM((count, width), bf16),
            pltpu.VMEM((1, width), jnp.float32),
            pltpu.VMEM((top_count, count), jnp.int32),
            pltpu.VMEM((top_count, count), jnp.float32),
            pltpu.VMEM(stored_keys.shape, bf16),
            pltpu.VMEM(stored_values.shape, bf16),
            pltpu.VMEM(w_gate.shape[1:], bf16),
            pltpu.VMEM(w_up.shape[1:], bf16),
            pltpu.VMEM(w_down.shape[1:], bf16),
            pltpu.VMEM((count, width), jnp.float32),
            pltpu.VMEM((devices * count, width + LANES), bf16),
            pltpu.VMEM((6 * count, hidden_units), bf16),
            pltpu.VMEM((devices * count, width), bf16),
            pltpu.VMEM((devices * count // 2, width), bf16),
            pltpu.VMEM((2, hops, count, width), bf16),
            pltpu.VMEM((2, hops, count, width), bf16),
            dma((5,)),
            dma((count // GROUP, 2)),
            dma((3,)),
            dma((hops, 2, 2)),
            dma((hops, 2, 2)),
            dma((hops + 1, 2, 2)),
            dma((hops + 1, 2, 2)),
            dma((hops + 1,)),
            dma((hops + 1,)),
            dma((hops, 2, 2)),
            dma((hops, 2, 2)),
        ],
        compiler_params=pltpu.CompilerParams(
            collective_id=0, has_side_effects=True, vmem_limit_bytes=60 * 1024 * 1024
        ),
        name="gathered_layer",
    )(
        hidden_in,
        queries,
        stored_lengths,
        norm_gain[None, :],
        expert_ids.T,
        gate_weights.T,
        stored_keys,
        stored_values,
        w_gate,
        w_up,
        w_down,
    ).astype(bf16)


def gather_suits(devices, local_experts, count, top_count):
    return (
        local_experts == 1
        and devices % 8 == 0
        and 2 * devices <= LANES
        and count % 32 == 0
        and count <= LANES
        and 2 * top_count >= devices
    )


def local(
    hidden_in,
    queries,
    stored_keys,
    stored_values,
    stored_lengths,
    norm_gain,
    expert_ids,
    gate_weights,
    w_gate,
    w_up,
    w_down,
):
    devices = lax.axis_size("ep")
    if gather_suits(devices, w_gate.shape[0], hidden_in.shape[0], expert_ids.shape[1]):
        return gathered_layer(
            hidden_in,
            queries,
            stored_keys,
            stored_values,
            stored_lengths,
            norm_gain,
            expert_ids,
            gate_weights,
            w_gate,
            w_up,
            w_down,
        )
    experts = devices * w_gate.shape[0]
    top_count = expert_ids.shape[1]
    capacity = max(2, 3 * MB_ROWS * top_count // (2 * experts))
    return layer_rows(
        hidden_in,
        queries,
        stored_keys,
        stored_values,
        stored_lengths,
        norm_gain,
        expert_ids,
        gate_weights,
        w_gate,
        w_up,
        w_down,
        MB * capacity,
    )


def solution(mesh):
    in_specs = (
        P(("groups", "ep"), None),
        P(("groups", "ep"), None),
        P(("groups", "ep"), None, None),
        P(("groups", "ep"), None, None),
        P(("groups", "ep")),
        P(),
        P(("groups", "ep"), None),
        P(("groups", "ep"), None),
        P("ep", None, None),
        P("ep", None, None),
        P("ep", None, None),
    )
    out_specs = P(("groups", "ep"), None)
    return jax.shard_map(local, mesh=mesh, in_specs=in_specs, out_specs=out_specs, check_vma=False)
```

```python
import functools
import math

import jax
import jax.numpy as jnp
from jax import lax
from jax.experimental import pallas as pl
from jax.experimental.pallas import tpu as pltpu
from jax.sharding import PartitionSpec as P

QUERY_HEADS = 16
KEY_VALUE_HEADS = 2
MB = 2
MB_ROWS = 16


def cached_attention(queries, stored_keys, stored_values, stored_lengths, heads, kv_heads):
    row_count = queries.shape[0]
    slots = stored_keys.shape[1]
    head_size = queries.shape[1] // heads
    query_head_rows = queries.reshape(row_count, kv_heads, heads // kv_heads, head_size)
    key_head_rows = stored_keys.reshape(row_count, slots, kv_heads, head_size)
    value_head_rows = stored_values.reshape(row_count, slots, kv_heads, head_size)
    scores = jnp.einsum(
        "nkgd,nckd->nkgc", query_head_rows, key_head_rows, preferred_element_type=jnp.float32
    ) / math.sqrt(head_size)
    visible = jnp.arange(slots, dtype=jnp.int32)[None, :] < stored_lengths[:, None]
    visible = visible[:, None, None, :]
    scores = jnp.where(visible, scores, -1e30)
    top_score = jnp.max(scores, axis=-1, keepdims=True)
    expo = jnp.where(visible, jnp.exp(scores - top_score), 0.0)
    probs = (expo / jnp.sum(expo, axis=-1, keepdims=True)).astype(jnp.bfloat16)
    attention_output = jnp.einsum(
        "nkgc,nckd->nkgd", probs, value_head_rows, preferred_element_type=jnp.float32
    )
    return attention_output.reshape(row_count, heads * head_size)


def expert_work(blocks, w_gate, w_up, w_down):
    gate_part = jnp.einsum("secd,edf->secf", blocks, w_gate, preferred_element_type=jnp.float32)
    up_part = jnp.einsum("secd,edf->secf", blocks, w_up, preferred_element_type=jnp.float32)
    inner = (jax.nn.silu(gate_part) * up_part).astype(jnp.bfloat16)
    return jnp.einsum("secf,efd->secd", inner, w_down, preferred_element_type=jnp.float32).astype(
        jnp.bfloat16
    )


def routed(normed, expert_ids, gate_weights, w_gate, w_up, w_down, capacity):
    devices = lax.axis_size("ep")
    local_count = w_gate.shape[0]
    experts = devices * local_count
    width = normed.shape[1]
    row_count, top_count = expert_ids.shape
    flat_ids = expert_ids.reshape(-1)
    onehot_table = (flat_ids[:, None] == jnp.arange(experts, dtype=jnp.int32)[None, :]).astype(
        jnp.int32
    )
    before = jnp.cumsum(onehot_table, axis=0) - onehot_table
    slot_index = jnp.sum(before * onehot_table, axis=1)
    target = flat_ids * capacity + slot_index
    target_rows = target.reshape(row_count, top_count)
    placing = jnp.sum(
        (
            target_rows[:, :, None]
            == jnp.arange(experts * capacity, dtype=jnp.int32)[None, None, :]
        ).astype(jnp.float32),
        axis=1,
    ).astype(jnp.bfloat16)
    buffer = jnp.einsum("tp,td->pd", placing, normed, preferred_element_type=jnp.float32).astype(
        jnp.bfloat16
    )
    buffer = buffer.reshape(experts, capacity, width)
    arrived = lax.all_to_all(buffer, "ep", split_axis=0, concat_axis=0, tiled=True)
    item_count = arrived.shape[1]
    blocks = arrived.reshape(devices, local_count, item_count, width)
    finished = expert_work(blocks, w_gate, w_up, w_down).reshape(experts, item_count, width)
    results = lax.all_to_all(finished, "ep", split_axis=0, concat_axis=0, tiled=True)
    picked = jnp.take(results.reshape(experts * capacity, width), target, axis=0)
    picked = picked.reshape(row_count, top_count, width).astype(jnp.float32)
    return jnp.sum(picked * gate_weights[:, :, None], axis=1)


def layer_rows(
    hidden_in,
    queries,
    stored_keys,
    stored_values,
    stored_lengths,
    norm_gain,
    expert_ids,
    gate_weights,
    w_gate,
    w_up,
    w_down,
    capacity,
):
    attention_output = cached_attention(
        queries, stored_keys, stored_values, stored_lengths, QUERY_HEADS, KEY_VALUE_HEADS
    )
    resid = hidden_in.astype(jnp.float32) + attention_output
    mean_square = jnp.mean(resid * resid, axis=-1, keepdims=True)
    normed = (resid * lax.rsqrt(mean_square + 1e-06) * norm_gain[None, :]).astype(jnp.bfloat16)
    mixture = routed(normed, expert_ids, gate_weights, w_gate, w_up, w_down, capacity)
    return (resid + mixture).astype(jnp.bfloat16)


LANES = 128
GROUP = 8


def chip_at(position, chips):
    half = chips // 2
    return jnp.where(position < half, 2 * position, 2 * (chips - 1 - position) + 1)


def position_of(chip, chips):
    return jnp.where(lax.rem(chip, 2) == 0, chip // 2, chips - 1 - chip // 2)


def tile_of(extent, most):
    return max(t for t in range(LANES, most + 1, LANES) if extent % t == 0)


def layer_kernel(
    devices,
    heads,
    kv_heads,
    hidden_hbm,
    queries_hbm,
    lengths_ref,
    gain_hbm,
    ids_hbm,
    weights_hbm,
    keys_hbm,
    values_hbm,
    gate_hbm,
    up_hbm,
    down_hbm,
    out_ref,
    hidden_ref,
    queries_ref,
    gain_ref,
    ids_ref,
    weights_ref,
    keys_ref,
    values_ref,
    gate_ref,
    up_ref,
    down_ref,
    resid_ref,
    rows_ref,
    inner_ref,
    own_ref,
    sibling_ref,
    outgoing_ref,
    incoming_ref,
    small_sem,
    kv_sem,
    w_sem,
    ring_send,
    ring_recv,
    pair_send,
    pair_recv,
    back_pair_send,
    back_pair_recv,
    back_send,
    back_recv,
):
    chips = devices // 2
    hops = chips // 2
    count, width = hidden_ref.shape
    slots = keys_ref.shape[1]
    head_size = width // heads
    per_kv = heads // kv_heads
    half = count // 2
    top_count = ids_ref.shape[0]
    hidden_units = gate_ref.shape[1]

    me = lax.axis_index("ep")
    core = lax.rem(me, 2)
    position = position_of(me // 2, chips)
    right = chip_at(lax.rem(position + 1, chips), chips) * 2 + core
    left = chip_at(lax.rem(position + chips - 1, chips), chips) * 2 + core
    sibling = me + 1 - 2 * core
    onward = (right, left)

    small_copies = []
    for j, (src, dst) in enumerate(
        (
            (queries_hbm, queries_ref),
            (hidden_hbm, hidden_ref),
            (gain_hbm, gain_ref),
            (ids_hbm, ids_ref),
            (weights_hbm, weights_ref),
        )
    ):
        copy = pltpu.make_async_copy(src, dst, small_sem.at[j])
        copy.start()
        small_copies.append(copy)
    groups = count // GROUP
    kv_copies = []
    for i in range(groups):
        part = pl.ds(i * GROUP, GROUP)
        for j, (src, dst) in enumerate(((keys_hbm, keys_ref), (values_hbm, values_ref))):
            copy = pltpu.make_async_copy(src.at[part], dst.at[part], kv_sem.at[i, j])
            copy.start()
            kv_copies.append(copy)
    barrier = pltpu.get_barrier_semaphore()
    others = [left, right, sibling]
    for other in others:
        pl.semaphore_signal(
            barrier, inc=1, device_id={"ep": other}, device_id_type=pl.DeviceIdType.MESH
        )
    for copy in small_copies:
        copy.wait()

    scale = 1.0 / math.sqrt(head_size)
    square_rows = per_kv * GROUP
    row_id = lax.broadcasted_iota(jnp.int32, (square_rows, GROUP * slots), 0)
    col_id = lax.broadcasted_iota(jnp.int32, (square_rows, GROUP * slots), 1)
    column_request = col_id // slots
    same_request = (row_id % GROUP) == column_request
    slot_id = col_id % slots
    def attend(i):
        part = pl.ds(i * GROUP, GROUP)
        lengths = jnp.zeros((square_rows, GROUP * slots), jnp.int32)
        for r in range(GROUP):
            lengths = jnp.where(column_request == r, lengths_ref[i * GROUP + r], lengths)
        visible = same_request & (slot_id < lengths)
        group_queries = queries_ref[part, :].astype(jnp.float32)
        hidden = hidden_ref[part, :].astype(jnp.float32)
        for g in range(kv_heads):
            lanes = slice(g * head_size, (g + 1) * head_size)
            first = g * per_kv
            q = jnp.concatenate(
                [
                    group_queries[:, (first + h) * head_size : (first + h + 1) * head_size]
                    for h in range(per_kv)
                ],
                axis=0,
            ).astype(jnp.bfloat16)
            k = keys_ref[part, :, lanes].reshape(GROUP * slots, head_size)
            v = values_ref[part, :, lanes].reshape(GROUP * slots, head_size)
            scores = (
                lax.dot_general(q, k, (((1,), (1,)), ((), ())), preferred_element_type=jnp.float32)
                * scale
            )
            scores = jnp.where(visible, scores, -1e30)
            expo = jnp.exp(scores - jnp.max(scores, axis=-1, keepdims=True))
            probs = (expo * (1.0 / jnp.sum(expo, axis=-1, keepdims=True))).astype(jnp.bfloat16)
            attended = jnp.dot(probs, v, preferred_element_type=jnp.float32)
            for h in range(per_kv):
                cols = slice((first + h) * head_size, (first + h + 1) * head_size)
                resid_ref[part, cols] = hidden[:, cols] + attended[h * GROUP : (h + 1) * GROUP, :]

    spare = LANES - count
    ids = jnp.concatenate([ids_ref[...], jnp.zeros((top_count, spare), jnp.int32)], axis=1)
    weights = jnp.concatenate([weights_ref[...], jnp.zeros((top_count, spare), jnp.float32)], axis=1)
    expert_id = lax.broadcasted_iota(jnp.int32, (LANES, LANES), 0)
    turned = jnp.zeros((LANES, LANES), jnp.float32)
    for k in range(top_count):
        chosen = ids[k : k + 1, :]
        turned = turned + jnp.where(
            (expert_id == chosen) | (expert_id == chosen + devices), weights[k : k + 1, :], 0.0
        )
    table = turned.T[0:count, :]
    lane = lax.broadcasted_iota(jnp.int32, (count, LANES), 1)
    coarse = table.astype(jnp.bfloat16)
    fine = (table - coarse.astype(jnp.float32)).astype(jnp.bfloat16)
    rows_ref[0:count, width : width + LANES] = jnp.where(
        lane < devices, coarse.astype(jnp.float32), fine.astype(jnp.float32)
    ).astype(jnp.bfloat16)

    def normalize(h):
        part = pl.ds(h * half, half)
        resid = resid_ref[part, :]
        mean_square = jnp.mean(resid * resid, axis=-1, keepdims=True)
        rows_ref[part, 0:width] = (
            resid * lax.rsqrt(mean_square + 1e-06) * gain_ref[...]
        ).astype(jnp.bfloat16)

    def chunk(s):
        return 0 if s == 0 else 2 * count + (s - 1) * 4 * count

    def own_rows(s):
        return 0 if s == 0 else count + (s - 1) * 2 * count

    def half_at(s, direction, h):
        if s in (0, hops):
            return chunk(s) + h * half
        return chunk(s) + direction * count + h * half

    def remote(src, dst, send, recv, other):
        return pltpu.make_async_remote_copy(
            src_ref=src,
            dst_ref=dst,
            send_sem=send,
            recv_sem=recv,
            device_id={"ep": other},
            device_id_type=pl.DeviceIdType.MESH,
        )

    def travels(s, direction, h):
        return s < hops or h == direction

    def ring_copy(s, direction, h):
        source = half_at(s - 1, direction, h)
        return remote(
            rows_ref.at[pl.ds(source, half)],
            rows_ref.at[pl.ds(half_at(s, direction, h), half)],
            ring_send.at[s - 1, direction, h],
            ring_recv.at[s - 1, direction, h],
            onward[direction],
        )

    def pair_copy(s, direction, h):
        start = half_at(s, direction, h)
        size = count if s in (0, hops) else 2 * count
        return remote(
            rows_ref.at[pl.ds(start, half)],
            rows_ref.at[pl.ds(start + size, half)],
            pair_send.at[s, direction, h],
            pair_recv.at[s, direction, h],
            sibling,
        )

    sent = []

    def go(copy):
        copy.start()
        sent.append(copy)

    def home(h):
        return pair_copy(0, 0, h)

    w_copies = []
    for h in range(2):
        for copy in kv_copies[h * groups : (h + 1) * groups]:
            copy.wait()
        for i in range(h * groups // 2, (h + 1) * groups // 2):
            attend(i)
        normalize(h)
        if h == 0:
            pl.semaphore_wait(barrier, len(others))
        for direction in range(2):
            go(ring_copy(1, direction, h))
        go(home(h))
        if h == 0:
            for j, (src, dst) in enumerate(((gate_hbm, gate_ref), (up_hbm, up_ref), (down_hbm, down_ref))):
                copy = pltpu.make_async_copy(src.at[0], dst, w_sem.at[j])
                copy.start()
                w_copies.append(copy)

    f_tile = tile_of(hidden_units, 256)
    d_tile = tile_of(width, 512)

    def expert(start, size):
        span = pl.ds(start, size)

        def first(i):
            cols = slice(i * f_tile, (i + 1) * f_tile)
            x = rows_ref[span, 0:width]
            gate = jnp.dot(x, gate_ref[:, cols], preferred_element_type=jnp.float32)
            up = jnp.dot(x, up_ref[:, cols], preferred_element_type=jnp.float32)
            inner_ref[0:size, cols] = (gate / (1.0 + jnp.exp(-gate)) * up).astype(jnp.bfloat16)

        def second(i):
            cols = slice(i * d_tile, (i + 1) * d_tile)
            spot = lax.broadcasted_iota(jnp.int32, (size, LANES), 1)
            both = rows_ref[span, width : width + LANES].astype(jnp.float32)
            weight = jnp.sum(
                jnp.where((spot == me) | (spot == me + devices), both, 0.0), axis=-1, keepdims=True
            )
            result = jnp.dot(
                inner_ref[0:size, :], down_ref[:, cols], preferred_element_type=jnp.float32
            )
            own_ref[span, cols] = (result * weight).astype(jnp.bfloat16)

        steps = [functools.partial(first, i) for i in range(hidden_units // f_tile)]
        return steps + [functools.partial(second, i) for i in range(width // d_tile)]

    def back_pair(s):
        size = count if s in (0, hops) else 2 * count
        return remote(
            own_ref.at[pl.ds(chunk(s) + size, size)],
            sibling_ref.at[pl.ds(own_rows(s), size)],
            back_pair_send.at[s],
            back_pair_recv.at[s],
            sibling,
        )

    pending = []

    def run(amount):
        for _ in range(min(amount, len(pending))):
            pending.pop(0)()

    def arrived(s):
        if s == 0:
            for h in range(2):
                home(h).wait_recv()
        for h in range(2):
            for direction in range(2):
                if s > 0 and travels(s, direction, h):
                    pair_copy(s, direction, h).wait_recv()

    def work(first, last):
        for s in range(first, last + 1):
            arrived(s)
        end = chunk(last) + (2 if last in (0, hops) else 4) * count
        pending.extend(expert(chunk(first), end - chunk(first)))
        for s in range(first, last + 1):
            pending.append(lambda s=s: go(back_pair(s)))

    for s in range(1, hops + 1):
        for h in range(2):
            for direction in range(2):
                if travels(s, direction, h):
                    ring_copy(s, direction, h).wait_recv()
                    if s < hops and travels(s + 1, direction, h):
                        go(ring_copy(s + 1, direction, h))
                    go(pair_copy(s, direction, h))
        if s == hops - 1:
            for copy in w_copies:
                copy.wait()
            for first in range(2, hops, 2):
                work(first, min(first + 1, hops - 1))
                run(len(pending))
    work(hops, hops)
    run(len(pending))
    work(0, 1)

    def back_copy(s, direction, h):
        return remote(
            outgoing_ref.at[direction, s - 1, pl.ds(h * half, half)],
            incoming_ref.at[direction, s - 1, pl.ds(h * half, half)],
            back_send.at[s - 1, direction, h],
            back_recv.at[s - 1, direction, h],
            onward[1 - direction],
        )

    def pass_back(s, direction, h):
        start = half_at(s, direction, h)
        offset = start - chunk(s) + own_rows(s)
        total = own_ref[pl.ds(start, half), :].astype(jnp.float32) + sibling_ref[
            pl.ds(offset, half), :
        ].astype(jnp.float32)
        if s < hops and travels(s + 1, direction, h):
            back_copy(s + 1, direction, h).wait_recv()
            total = total + incoming_ref[direction, s, pl.ds(h * half, half), :].astype(jnp.float32)
        outgoing_ref[direction, s - 1, pl.ds(h * half, half), :] = total.astype(jnp.bfloat16)
        go(back_copy(s, direction, h))

    for s in range(hops, 0, -1):
        if s == hops:
            back_pair(s).wait_recv()
        for direction in range(2):
            pass_back(s, direction, direction)
        if s > 1:
            if s == 2:
                run(len(pending))
            back_pair(s - 1).wait_recv()
            for direction in range(2):
                pass_back(s - 1, direction, 1 - direction)
            run(3)

    back_pair(0).wait_recv()
    for h in range(2):
        span = pl.ds(h * half, half)
        total = own_ref[span, :].astype(jnp.float32) + sibling_ref[span, :].astype(jnp.float32)
        total = total + resid_ref[span, :]
        for direction in range(2):
            back_copy(1, direction, h).wait_recv()
            total = total + incoming_ref[direction, 0, span, :].astype(jnp.float32)
        out_ref[span, :] = total

    for copy in sent:
        copy.wait_send()


def gathered_layer(
    hidden_in,
    queries,
    stored_keys,
    stored_values,
    stored_lengths,
    norm_gain,
    expert_ids,
    gate_weights,
    w_gate,
    w_up,
    w_down,
):
    devices = lax.axis_size("ep")
    count, width = hidden_in.shape
    hidden_units = w_gate.shape[2]
    hops = devices // 4
    vmem = pl.BlockSpec(memory_space=pltpu.VMEM)
    smem = pl.BlockSpec(memory_space=pltpu.SMEM)
    hbm = pl.BlockSpec(memory_space=pltpu.HBM)
    dma = pltpu.SemaphoreType.DMA
    bf16 = jnp.bfloat16
    top_count = expert_ids.shape[1]
    return pl.pallas_call(
        functools.partial(layer_kernel, devices, QUERY_HEADS, KEY_VALUE_HEADS),
        out_shape=jax.ShapeDtypeStruct((count, width), jnp.float32),
        in_specs=[hbm, hbm, smem] + [hbm] * 8,
        out_specs=vmem,
        scratch_shapes=[
            pltpu.VMEM((count, width), bf16),
            pltpu.VMEM((count, width), bf16),
            pltpu.VMEM((1, width), jnp.float32),
            pltpu.VMEM((top_count, count), jnp.int32),
            pltpu.VMEM((top_count, count), jnp.float32),
            pltpu.VMEM(stored_keys.shape, bf16),
            pltpu.VMEM(stored_values.shape, bf16),
            pltpu.VMEM(w_gate.shape[1:], bf16),
            pltpu.VMEM(w_up.shape[1:], bf16),
            pltpu.VMEM(w_down.shape[1:], bf16),
            pltpu.VMEM((count, width), jnp.float32),
            pltpu.VMEM((devices * count, width + LANES), bf16),
            pltpu.VMEM((8 * count, hidden_units), bf16),
            pltpu.VMEM((devices * count, width), bf16),
            pltpu.VMEM((devices * count // 2, width), bf16),
            pltpu.VMEM((2, hops, count, width), bf16),
            pltpu.VMEM((2, hops, count, width), bf16),
            dma((5,)),
            dma((count // GROUP, 2)),
            dma((3,)),
            dma((hops, 2, 2)),
            dma((hops, 2, 2)),
            dma((hops + 1, 2, 2)),
            dma((hops + 1, 2, 2)),
            dma((hops + 1,)),
            dma((hops + 1,)),
            dma((hops, 2, 2)),
            dma((hops, 2, 2)),
        ],
        compiler_params=pltpu.CompilerParams(
            collective_id=0, has_side_effects=True, vmem_limit_bytes=60 * 1024 * 1024
        ),
        name="gathered_layer",
    )(
        hidden_in,
        queries,
        stored_lengths,
        norm_gain[None, :],
        expert_ids.T,
        gate_weights.T,
        stored_keys,
        stored_values,
        w_gate,
        w_up,
        w_down,
    ).astype(bf16)


def gather_suits(devices, local_experts, count, top_count):
    return (
        local_experts == 1
        and devices % 8 == 0
        and 2 * devices <= LANES
        and count % 32 == 0
        and count <= LANES
        and 2 * top_count >= devices
    )


def local(
    hidden_in,
    queries,
    stored_keys,
    stored_values,
    stored_lengths,
    norm_gain,
    expert_ids,
    gate_weights,
    w_gate,
    w_up,
    w_down,
):
    devices = lax.axis_size("ep")
    if gather_suits(devices, w_gate.shape[0], hidden_in.shape[0], expert_ids.shape[1]):
        return gathered_layer(
            hidden_in,
            queries,
            stored_keys,
            stored_values,
            stored_lengths,
            norm_gain,
            expert_ids,
            gate_weights,
            w_gate,
            w_up,
            w_down,
        )
    experts = devices * w_gate.shape[0]
    top_count = expert_ids.shape[1]
    capacity = max(2, 3 * MB_ROWS * top_count // (2 * experts))
    return layer_rows(
        hidden_in,
        queries,
        stored_keys,
        stored_values,
        stored_lengths,
        norm_gain,
        expert_ids,
        gate_weights,
        w_gate,
        w_up,
        w_down,
        MB * capacity,
    )


def solution(mesh):
    in_specs = (
        P(("groups", "ep"), None),
        P(("groups", "ep"), None),
        P(("groups", "ep"), None, None),
        P(("groups", "ep"), None, None),
        P(("groups", "ep")),
        P(),
        P(("groups", "ep"), None),
        P(("groups", "ep"), None),
        P("ep", None, None),
        P("ep", None, None),
        P("ep", None, None),
    )
    out_specs = P(("groups", "ep"), None)
    return jax.shard_map(local, mesh=mesh, in_specs=in_specs, out_specs=out_specs, check_vma=False)
```

```python
import functools
import math

import jax
import jax.numpy as jnp
from jax import lax
from jax.experimental import pallas as pl
from jax.experimental.pallas import tpu as pltpu
from jax.sharding import PartitionSpec as P

QUERY_HEADS = 16
KEY_VALUE_HEADS = 2
MB = 2
MB_ROWS = 16


def cached_attention(queries, stored_keys, stored_values, stored_lengths, heads, kv_heads):
    row_count = queries.shape[0]
    slots = stored_keys.shape[1]
    head_size = queries.shape[1] // heads
    query_head_rows = queries.reshape(row_count, kv_heads, heads // kv_heads, head_size)
    key_head_rows = stored_keys.reshape(row_count, slots, kv_heads, head_size)
    value_head_rows = stored_values.reshape(row_count, slots, kv_heads, head_size)
    scores = jnp.einsum(
        "nkgd,nckd->nkgc", query_head_rows, key_head_rows, preferred_element_type=jnp.float32
    ) / math.sqrt(head_size)
    visible = jnp.arange(slots, dtype=jnp.int32)[None, :] < stored_lengths[:, None]
    visible = visible[:, None, None, :]
    scores = jnp.where(visible, scores, -1e30)
    top_score = jnp.max(scores, axis=-1, keepdims=True)
    expo = jnp.where(visible, jnp.exp(scores - top_score), 0.0)
    probs = (expo / jnp.sum(expo, axis=-1, keepdims=True)).astype(jnp.bfloat16)
    attention_output = jnp.einsum(
        "nkgc,nckd->nkgd", probs, value_head_rows, preferred_element_type=jnp.float32
    )
    return attention_output.reshape(row_count, heads * head_size)


def expert_work(blocks, w_gate, w_up, w_down):
    gate_part = jnp.einsum("secd,edf->secf", blocks, w_gate, preferred_element_type=jnp.float32)
    up_part = jnp.einsum("secd,edf->secf", blocks, w_up, preferred_element_type=jnp.float32)
    inner = (jax.nn.silu(gate_part) * up_part).astype(jnp.bfloat16)
    return jnp.einsum("secf,efd->secd", inner, w_down, preferred_element_type=jnp.float32).astype(
        jnp.bfloat16
    )


def routed(normed, expert_ids, gate_weights, w_gate, w_up, w_down, capacity):
    devices = lax.axis_size("ep")
    local_count = w_gate.shape[0]
    experts = devices * local_count
    width = normed.shape[1]
    row_count, top_count = expert_ids.shape
    flat_ids = expert_ids.reshape(-1)
    onehot_table = (flat_ids[:, None] == jnp.arange(experts, dtype=jnp.int32)[None, :]).astype(
        jnp.int32
    )
    before = jnp.cumsum(onehot_table, axis=0) - onehot_table
    slot_index = jnp.sum(before * onehot_table, axis=1)
    target = flat_ids * capacity + slot_index
    target_rows = target.reshape(row_count, top_count)
    placing = jnp.sum(
        (
            target_rows[:, :, None]
            == jnp.arange(experts * capacity, dtype=jnp.int32)[None, None, :]
        ).astype(jnp.float32),
        axis=1,
    ).astype(jnp.bfloat16)
    buffer = jnp.einsum("tp,td->pd", placing, normed, preferred_element_type=jnp.float32).astype(
        jnp.bfloat16
    )
    buffer = buffer.reshape(experts, capacity, width)
    arrived = lax.all_to_all(buffer, "ep", split_axis=0, concat_axis=0, tiled=True)
    item_count = arrived.shape[1]
    blocks = arrived.reshape(devices, local_count, item_count, width)
    finished = expert_work(blocks, w_gate, w_up, w_down).reshape(experts, item_count, width)
    results = lax.all_to_all(finished, "ep", split_axis=0, concat_axis=0, tiled=True)
    picked = jnp.take(results.reshape(experts * capacity, width), target, axis=0)
    picked = picked.reshape(row_count, top_count, width).astype(jnp.float32)
    return jnp.sum(picked * gate_weights[:, :, None], axis=1)


def layer_rows(
    hidden_in,
    queries,
    stored_keys,
    stored_values,
    stored_lengths,
    norm_gain,
    expert_ids,
    gate_weights,
    w_gate,
    w_up,
    w_down,
    capacity,
):
    attention_output = cached_attention(
        queries, stored_keys, stored_values, stored_lengths, QUERY_HEADS, KEY_VALUE_HEADS
    )
    resid = hidden_in.astype(jnp.float32) + attention_output
    mean_square = jnp.mean(resid * resid, axis=-1, keepdims=True)
    normed = (resid * lax.rsqrt(mean_square + 1e-06) * norm_gain[None, :]).astype(jnp.bfloat16)
    mixture = routed(normed, expert_ids, gate_weights, w_gate, w_up, w_down, capacity)
    return (resid + mixture).astype(jnp.bfloat16)


LANES = 128
GROUP = 8


def chip_at(position, chips):
    half = chips // 2
    return jnp.where(position < half, 2 * position, 2 * (chips - 1 - position) + 1)


def position_of(chip, chips):
    return jnp.where(lax.rem(chip, 2) == 0, chip // 2, chips - 1 - chip // 2)


def tile_of(extent, most):
    return max(t for t in range(LANES, most + 1, LANES) if extent % t == 0)


def layer_kernel(
    devices,
    heads,
    kv_heads,
    hidden_hbm,
    queries_hbm,
    lengths_ref,
    gain_hbm,
    ids_hbm,
    weights_hbm,
    keys_hbm,
    values_hbm,
    gate_hbm,
    up_hbm,
    down_hbm,
    out_ref,
    hidden_ref,
    queries_ref,
    gain_ref,
    ids_ref,
    weights_ref,
    keys_ref,
    values_ref,
    gate_ref,
    up_ref,
    down_ref,
    resid_ref,
    rows_ref,
    inner_ref,
    own_ref,
    sibling_ref,
    outgoing_ref,
    incoming_ref,
    small_sem,
    kv_sem,
    w_sem,
    ring_send,
    ring_recv,
    pair_send,
    pair_recv,
    back_pair_send,
    back_pair_recv,
    back_send,
    back_recv,
):
    chips = devices // 2
    hops = chips // 2
    count, width = hidden_ref.shape
    slots = keys_ref.shape[1]
    head_size = width // heads
    per_kv = heads // kv_heads
    half = count // 2
    top_count = ids_ref.shape[0]
    hidden_units = gate_ref.shape[1]

    me = lax.axis_index("ep")
    core = lax.rem(me, 2)
    position = position_of(me // 2, chips)
    right = chip_at(lax.rem(position + 1, chips), chips) * 2 + core
    left = chip_at(lax.rem(position + chips - 1, chips), chips) * 2 + core
    sibling = me + 1 - 2 * core
    onward = (right, left)

    small_copies = []
    for j, (src, dst) in enumerate(
        (
            (queries_hbm, queries_ref),
            (hidden_hbm, hidden_ref),
            (gain_hbm, gain_ref),
            (ids_hbm, ids_ref),
            (weights_hbm, weights_ref),
        )
    ):
        copy = pltpu.make_async_copy(src, dst, small_sem.at[j])
        copy.start()
        small_copies.append(copy)
    groups = count // GROUP
    kv_copies = []
    for i in range(groups):
        part = pl.ds(i * GROUP, GROUP)
        for j, (src, dst) in enumerate(((keys_hbm, keys_ref), (values_hbm, values_ref))):
            copy = pltpu.make_async_copy(src.at[part], dst.at[part], kv_sem.at[i, j])
            copy.start()
            kv_copies.append(copy)
    barrier = pltpu.get_barrier_semaphore()
    others = [left, right, sibling]
    for other in others:
        pl.semaphore_signal(
            barrier, inc=1, device_id={"ep": other}, device_id_type=pl.DeviceIdType.MESH
        )
    for copy in small_copies:
        copy.wait()

    scale = 1.0 / math.sqrt(head_size)
    square_rows = per_kv * GROUP
    row_id = lax.broadcasted_iota(jnp.int32, (square_rows, GROUP * slots), 0)
    col_id = lax.broadcasted_iota(jnp.int32, (square_rows, GROUP * slots), 1)
    column_request = col_id // slots
    same_request = (row_id % GROUP) == column_request
    slot_id = col_id % slots
    def attend(i):
        part = pl.ds(i * GROUP, GROUP)
        lengths = jnp.zeros((square_rows, GROUP * slots), jnp.int32)
        for r in range(GROUP):
            lengths = jnp.where(column_request == r, lengths_ref[i * GROUP + r], lengths)
        visible = same_request & (slot_id < lengths)
        group_queries = queries_ref[part, :].astype(jnp.float32)
        hidden = hidden_ref[part, :].astype(jnp.float32)
        for g in range(kv_heads):
            lanes = slice(g * head_size, (g + 1) * head_size)
            first = g * per_kv
            q = jnp.concatenate(
                [
                    group_queries[:, (first + h) * head_size : (first + h + 1) * head_size]
                    for h in range(per_kv)
                ],
                axis=0,
            ).astype(jnp.bfloat16)
            k = keys_ref[part, :, lanes].reshape(GROUP * slots, head_size)
            v = values_ref[part, :, lanes].reshape(GROUP * slots, head_size)
            scores = (
                lax.dot_general(q, k, (((1,), (1,)), ((), ())), preferred_element_type=jnp.float32)
                * scale
            )
            scores = jnp.where(visible, scores, -1e30)
            expo = jnp.exp(scores - jnp.max(scores, axis=-1, keepdims=True))
            probs = (expo * (1.0 / jnp.sum(expo, axis=-1, keepdims=True))).astype(jnp.bfloat16)
            attended = jnp.dot(probs, v, preferred_element_type=jnp.float32)
            for h in range(per_kv):
                cols = slice((first + h) * head_size, (first + h + 1) * head_size)
                resid_ref[part, cols] = hidden[:, cols] + attended[h * GROUP : (h + 1) * GROUP, :]

    spare = LANES - count
    ids = jnp.concatenate([ids_ref[...], jnp.zeros((top_count, spare), jnp.int32)], axis=1)
    weights = jnp.concatenate([weights_ref[...], jnp.zeros((top_count, spare), jnp.float32)], axis=1)
    expert_id = lax.broadcasted_iota(jnp.int32, (LANES, LANES), 0)
    turned = jnp.zeros((LANES, LANES), jnp.float32)
    for k in range(top_count):
        chosen = ids[k : k + 1, :]
        turned = turned + jnp.where(
            (expert_id == chosen) | (expert_id == chosen + devices), weights[k : k + 1, :], 0.0
        )
    table = turned.T[0:count, :]
    lane = lax.broadcasted_iota(jnp.int32, (count, LANES), 1)
    coarse = table.astype(jnp.bfloat16)
    fine = (table - coarse.astype(jnp.float32)).astype(jnp.bfloat16)
    rows_ref[0:count, width : width + LANES] = jnp.where(
        lane < devices, coarse.astype(jnp.float32), fine.astype(jnp.float32)
    ).astype(jnp.bfloat16)

    def normalize(h):
        part = pl.ds(h * half, half)
        resid = resid_ref[part, :]
        mean_square = jnp.mean(resid * resid, axis=-1, keepdims=True)
        rows_ref[part, 0:width] = (
            resid * lax.rsqrt(mean_square + 1e-06) * gain_ref[...]
        ).astype(jnp.bfloat16)

    def chunk(s):
        return 0 if s == 0 else 2 * count + (s - 1) * 4 * count

    def own_rows(s):
        return 0 if s == 0 else count + (s - 1) * 2 * count

    def half_at(s, direction, h):
        if s in (0, hops):
            return chunk(s) + h * half
        return chunk(s) + direction * count + h * half

    def remote(src, dst, send, recv, other):
        return pltpu.make_async_remote_copy(
            src_ref=src,
            dst_ref=dst,
            send_sem=send,
            recv_sem=recv,
            device_id={"ep": other},
            device_id_type=pl.DeviceIdType.MESH,
        )

    def travels(s, direction, h):
        return s < hops or h == direction

    split = width // 2 // LANES * LANES

    def part_of(c, end):
        return pl.ds(0, split) if c == 0 else pl.ds(split, end - split)

    def ring_copy(s, direction, h, c):
        cols = part_of(c, width + LANES)
        return remote(
            rows_ref.at[pl.ds(half_at(s - 1, direction, h), half), cols],
            rows_ref.at[pl.ds(half_at(s, direction, h), half), cols],
            ring_send.at[s - 1, direction, h, c],
            ring_recv.at[s - 1, direction, h, c],
            onward[direction],
        )

    def pair_copy(s, direction, h):
        start = half_at(s, direction, h)
        size = count if s in (0, hops) else 2 * count
        return remote(
            rows_ref.at[pl.ds(start, half)],
            rows_ref.at[pl.ds(start + size, half)],
            pair_send.at[s, direction, h],
            pair_recv.at[s, direction, h],
            sibling,
        )

    sent = []

    def go(copy):
        copy.start()
        sent.append(copy)

    def home(h):
        return pair_copy(0, 0, h)

    w_copies = []
    for h in range(2):
        for copy in kv_copies[h * groups : (h + 1) * groups]:
            copy.wait()
        for i in range(h * groups // 2, (h + 1) * groups // 2):
            attend(i)
        normalize(h)
        if h == 0:
            pl.semaphore_wait(barrier, len(others))
        for c in range(2):
            for direction in range(2):
                go(ring_copy(1, direction, h, c))
        go(home(h))
        if h == 0:
            for j, (src, dst) in enumerate(((gate_hbm, gate_ref), (up_hbm, up_ref), (down_hbm, down_ref))):
                copy = pltpu.make_async_copy(src.at[0], dst, w_sem.at[j])
                copy.start()
                w_copies.append(copy)

    f_tile = tile_of(hidden_units, 256)
    d_tile = tile_of(width, 512)

    def expert(start, size):
        span = pl.ds(start, size)

        def first(i):
            cols = slice(i * f_tile, (i + 1) * f_tile)
            x = rows_ref[span, 0:width]
            gate = jnp.dot(x, gate_ref[:, cols], preferred_element_type=jnp.float32)
            up = jnp.dot(x, up_ref[:, cols], preferred_element_type=jnp.float32)
            inner_ref[0:size, cols] = (gate / (1.0 + jnp.exp(-gate)) * up).astype(jnp.bfloat16)

        def second(i):
            cols = slice(i * d_tile, (i + 1) * d_tile)
            spot = lax.broadcasted_iota(jnp.int32, (size, LANES), 1)
            both = rows_ref[span, width : width + LANES].astype(jnp.float32)
            weight = jnp.sum(
                jnp.where((spot == me) | (spot == me + devices), both, 0.0), axis=-1, keepdims=True
            )
            result = jnp.dot(
                inner_ref[0:size, :], down_ref[:, cols], preferred_element_type=jnp.float32
            )
            own_ref[span, cols] = (result * weight).astype(jnp.bfloat16)

        steps = [functools.partial(first, i) for i in range(hidden_units // f_tile)]
        return steps + [functools.partial(second, i) for i in range(width // d_tile)]

    def back_pair(s):
        size = count if s in (0, hops) else 2 * count
        return remote(
            own_ref.at[pl.ds(chunk(s) + size, size)],
            sibling_ref.at[pl.ds(own_rows(s), size)],
            back_pair_send.at[s],
            back_pair_recv.at[s],
            sibling,
        )

    pending = []

    def run(amount):
        for _ in range(min(amount, len(pending))):
            pending.pop(0)()

    def arrived(s):
        if s == 0:
            for h in range(2):
                home(h).wait_recv()
        for h in range(2):
            for direction in range(2):
                if s > 0 and travels(s, direction, h):
                    pair_copy(s, direction, h).wait_recv()

    def work(first, last):
        for s in range(first, last + 1):
            arrived(s)
        end = chunk(last) + (2 if last in (0, hops) else 4) * count
        pending.extend(expert(chunk(first), end - chunk(first)))
        for s in range(first, last + 1):
            pending.append(lambda s=s: go(back_pair(s)))

    for s in range(1, hops + 1):
        for h in range(2):
            for c in range(2):
                for direction in range(2):
                    if travels(s, direction, h):
                        ring_copy(s, direction, h, c).wait_recv()
                        if s < hops and travels(s + 1, direction, h):
                            go(ring_copy(s + 1, direction, h, c))
                        if c == 1:
                            go(pair_copy(s, direction, h))
        if s == hops - 1:
            for copy in w_copies:
                copy.wait()
            for first in range(2, hops, 2):
                work(first, min(first + 1, hops - 1))
                run(len(pending))
    work(hops, hops)
    run(len(pending))
    work(0, 1)

    def back_copy(s, direction, h, c):
        spot = (direction, s - 1, pl.ds(h * half, half), part_of(c, width))
        return remote(
            outgoing_ref.at[spot],
            incoming_ref.at[spot],
            back_send.at[s - 1, direction, h, c],
            back_recv.at[s - 1, direction, h, c],
            onward[1 - direction],
        )

    def pass_back(s, direction, h, c):
        cols = part_of(c, width)
        start = half_at(s, direction, h)
        offset = start - chunk(s) + own_rows(s)
        total = own_ref[pl.ds(start, half), cols].astype(jnp.float32) + sibling_ref[
            pl.ds(offset, half), cols
        ].astype(jnp.float32)
        if s < hops and travels(s + 1, direction, h):
            back_copy(s + 1, direction, h, c).wait_recv()
            total = total + incoming_ref[direction, s, pl.ds(h * half, half), cols].astype(
                jnp.float32
            )
        outgoing_ref[direction, s - 1, pl.ds(h * half, half), cols] = total.astype(jnp.bfloat16)
        go(back_copy(s, direction, h, c))

    for s in range(hops, 0, -1):
        if s == hops:
            back_pair(s).wait_recv()
        for c in range(2):
            for direction in range(2):
                pass_back(s, direction, direction, c)
        if s > 1:
            if s == 2:
                run(len(pending))
            back_pair(s - 1).wait_recv()
            for c in range(2):
                for direction in range(2):
                    pass_back(s - 1, direction, 1 - direction, c)
            run(3)

    back_pair(0).wait_recv()
    for h in range(2):
        span = pl.ds(h * half, half)
        total = own_ref[span, :].astype(jnp.float32) + sibling_ref[span, :].astype(jnp.float32)
        total = total + resid_ref[span, :]
        for direction in range(2):
            for c in range(2):
                back_copy(1, direction, h, c).wait_recv()
            total = total + incoming_ref[direction, 0, span, :].astype(jnp.float32)
        out_ref[span, :] = total

    for copy in sent:
        copy.wait_send()


def gathered_layer(
    hidden_in,
    queries,
    stored_keys,
    stored_values,
    stored_lengths,
    norm_gain,
    expert_ids,
    gate_weights,
    w_gate,
    w_up,
    w_down,
):
    devices = lax.axis_size("ep")
    count, width = hidden_in.shape
    hidden_units = w_gate.shape[2]
    hops = devices // 4
    vmem = pl.BlockSpec(memory_space=pltpu.VMEM)
    smem = pl.BlockSpec(memory_space=pltpu.SMEM)
    hbm = pl.BlockSpec(memory_space=pltpu.HBM)
    dma = pltpu.SemaphoreType.DMA
    bf16 = jnp.bfloat16
    top_count = expert_ids.shape[1]
    return pl.pallas_call(
        functools.partial(layer_kernel, devices, QUERY_HEADS, KEY_VALUE_HEADS),
        out_shape=jax.ShapeDtypeStruct((count, width), jnp.float32),
        in_specs=[hbm, hbm, smem] + [hbm] * 8,
        out_specs=vmem,
        scratch_shapes=[
            pltpu.VMEM((count, width), bf16),
            pltpu.VMEM((count, width), bf16),
            pltpu.VMEM((1, width), jnp.float32),
            pltpu.VMEM((top_count, count), jnp.int32),
            pltpu.VMEM((top_count, count), jnp.float32),
            pltpu.VMEM(stored_keys.shape, bf16),
            pltpu.VMEM(stored_values.shape, bf16),
            pltpu.VMEM(w_gate.shape[1:], bf16),
            pltpu.VMEM(w_up.shape[1:], bf16),
            pltpu.VMEM(w_down.shape[1:], bf16),
            pltpu.VMEM((count, width), jnp.float32),
            pltpu.VMEM((devices * count, width + LANES), bf16),
            pltpu.VMEM((8 * count, hidden_units), bf16),
            pltpu.VMEM((devices * count, width), bf16),
            pltpu.VMEM((devices * count // 2, width), bf16),
            pltpu.VMEM((2, hops, count, width), bf16),
            pltpu.VMEM((2, hops, count, width), bf16),
            dma((5,)),
            dma((count // GROUP, 2)),
            dma((3,)),
            dma((hops, 2, 2, 2)),
            dma((hops, 2, 2, 2)),
            dma((hops + 1, 2, 2)),
            dma((hops + 1, 2, 2)),
            dma((hops + 1,)),
            dma((hops + 1,)),
            dma((hops, 2, 2, 2)),
            dma((hops, 2, 2, 2)),
        ],
        compiler_params=pltpu.CompilerParams(
            collective_id=0, has_side_effects=True, vmem_limit_bytes=60 * 1024 * 1024
        ),
        name="gathered_layer",
    )(
        hidden_in,
        queries,
        stored_lengths,
        norm_gain[None, :],
        expert_ids.T,
        gate_weights.T,
        stored_keys,
        stored_values,
        w_gate,
        w_up,
        w_down,
    ).astype(bf16)


def gather_suits(devices, local_experts, count, top_count):
    return (
        local_experts == 1
        and devices % 8 == 0
        and 2 * devices <= LANES
        and count % 32 == 0
        and count <= LANES
        and 2 * top_count >= devices
    )


def local(
    hidden_in,
    queries,
    stored_keys,
    stored_values,
    stored_lengths,
    norm_gain,
    expert_ids,
    gate_weights,
    w_gate,
    w_up,
    w_down,
):
    devices = lax.axis_size("ep")
    if gather_suits(devices, w_gate.shape[0], hidden_in.shape[0], expert_ids.shape[1]):
        return gathered_layer(
            hidden_in,
            queries,
            stored_keys,
            stored_values,
            stored_lengths,
            norm_gain,
            expert_ids,
            gate_weights,
            w_gate,
            w_up,
            w_down,
        )
    experts = devices * w_gate.shape[0]
    top_count = expert_ids.shape[1]
    capacity = max(2, 3 * MB_ROWS * top_count // (2 * experts))
    return layer_rows(
        hidden_in,
        queries,
        stored_keys,
        stored_values,
        stored_lengths,
        norm_gain,
        expert_ids,
        gate_weights,
        w_gate,
        w_up,
        w_down,
        MB * capacity,
    )


def solution(mesh):
    in_specs = (
        P(("groups", "ep"), None),
        P(("groups", "ep"), None),
        P(("groups", "ep"), None, None),
        P(("groups", "ep"), None, None),
        P(("groups", "ep")),
        P(),
        P(("groups", "ep"), None),
        P(("groups", "ep"), None),
        P("ep", None, None),
        P("ep", None, None),
        P("ep", None, None),
    )
    out_specs = P(("groups", "ep"), None)
    return jax.shard_map(local, mesh=mesh, in_specs=in_specs, out_specs=out_specs, check_vma=False)
```

```python
import functools
import math

import jax
import jax.numpy as jnp
from jax import lax
from jax.experimental import pallas as pl
from jax.experimental.pallas import tpu as pltpu
from jax.sharding import PartitionSpec as P

QUERY_HEADS = 16
KEY_VALUE_HEADS = 2
MB = 2
MB_ROWS = 16


def cached_attention(queries, stored_keys, stored_values, stored_lengths, heads, kv_heads):
    row_count = queries.shape[0]
    slots = stored_keys.shape[1]
    head_size = queries.shape[1] // heads
    query_head_rows = queries.reshape(row_count, kv_heads, heads // kv_heads, head_size)
    key_head_rows = stored_keys.reshape(row_count, slots, kv_heads, head_size)
    value_head_rows = stored_values.reshape(row_count, slots, kv_heads, head_size)
    scores = jnp.einsum(
        "nkgd,nckd->nkgc", query_head_rows, key_head_rows, preferred_element_type=jnp.float32
    ) / math.sqrt(head_size)
    visible = jnp.arange(slots, dtype=jnp.int32)[None, :] < stored_lengths[:, None]
    visible = visible[:, None, None, :]
    scores = jnp.where(visible, scores, -1e30)
    top_score = jnp.max(scores, axis=-1, keepdims=True)
    expo = jnp.where(visible, jnp.exp(scores - top_score), 0.0)
    probs = (expo / jnp.sum(expo, axis=-1, keepdims=True)).astype(jnp.bfloat16)
    attention_output = jnp.einsum(
        "nkgc,nckd->nkgd", probs, value_head_rows, preferred_element_type=jnp.float32
    )
    return attention_output.reshape(row_count, heads * head_size)


def expert_work(blocks, w_gate, w_up, w_down):
    gate_part = jnp.einsum("secd,edf->secf", blocks, w_gate, preferred_element_type=jnp.float32)
    up_part = jnp.einsum("secd,edf->secf", blocks, w_up, preferred_element_type=jnp.float32)
    inner = (jax.nn.silu(gate_part) * up_part).astype(jnp.bfloat16)
    return jnp.einsum("secf,efd->secd", inner, w_down, preferred_element_type=jnp.float32).astype(
        jnp.bfloat16
    )


def routed(normed, expert_ids, gate_weights, w_gate, w_up, w_down, capacity):
    devices = lax.axis_size("ep")
    local_count = w_gate.shape[0]
    experts = devices * local_count
    width = normed.shape[1]
    row_count, top_count = expert_ids.shape
    flat_ids = expert_ids.reshape(-1)
    onehot_table = (flat_ids[:, None] == jnp.arange(experts, dtype=jnp.int32)[None, :]).astype(
        jnp.int32
    )
    before = jnp.cumsum(onehot_table, axis=0) - onehot_table
    slot_index = jnp.sum(before * onehot_table, axis=1)
    target = flat_ids * capacity + slot_index
    target_rows = target.reshape(row_count, top_count)
    placing = jnp.sum(
        (
            target_rows[:, :, None]
            == jnp.arange(experts * capacity, dtype=jnp.int32)[None, None, :]
        ).astype(jnp.float32),
        axis=1,
    ).astype(jnp.bfloat16)
    buffer = jnp.einsum("tp,td->pd", placing, normed, preferred_element_type=jnp.float32).astype(
        jnp.bfloat16
    )
    buffer = buffer.reshape(experts, capacity, width)
    arrived = lax.all_to_all(buffer, "ep", split_axis=0, concat_axis=0, tiled=True)
    item_count = arrived.shape[1]
    blocks = arrived.reshape(devices, local_count, item_count, width)
    finished = expert_work(blocks, w_gate, w_up, w_down).reshape(experts, item_count, width)
    results = lax.all_to_all(finished, "ep", split_axis=0, concat_axis=0, tiled=True)
    picked = jnp.take(results.reshape(experts * capacity, width), target, axis=0)
    picked = picked.reshape(row_count, top_count, width).astype(jnp.float32)
    return jnp.sum(picked * gate_weights[:, :, None], axis=1)


def layer_rows(
    hidden_in,
    queries,
    stored_keys,
    stored_values,
    stored_lengths,
    norm_gain,
    expert_ids,
    gate_weights,
    w_gate,
    w_up,
    w_down,
    capacity,
):
    attention_output = cached_attention(
        queries, stored_keys, stored_values, stored_lengths, QUERY_HEADS, KEY_VALUE_HEADS
    )
    resid = hidden_in.astype(jnp.float32) + attention_output
    mean_square = jnp.mean(resid * resid, axis=-1, keepdims=True)
    normed = (resid * lax.rsqrt(mean_square + 1e-06) * norm_gain[None, :]).astype(jnp.bfloat16)
    mixture = routed(normed, expert_ids, gate_weights, w_gate, w_up, w_down, capacity)
    return (resid + mixture).astype(jnp.bfloat16)


LANES = 128
GROUP = 8


def chip_at(position, chips):
    half = chips // 2
    return jnp.where(position < half, 2 * position, 2 * (chips - 1 - position) + 1)


def position_of(chip, chips):
    return jnp.where(lax.rem(chip, 2) == 0, chip // 2, chips - 1 - chip // 2)


def tile_of(extent, most):
    return max(t for t in range(LANES, most + 1, LANES) if extent % t == 0)


def layer_kernel(
    devices,
    heads,
    kv_heads,
    hidden_hbm,
    queries_hbm,
    lengths_ref,
    gain_hbm,
    ids_hbm,
    weights_hbm,
    keys_hbm,
    values_hbm,
    gate_hbm,
    up_hbm,
    down_hbm,
    out_ref,
    hidden_ref,
    queries_ref,
    gain_ref,
    ids_ref,
    weights_ref,
    keys_ref,
    values_ref,
    gate_ref,
    up_ref,
    down_ref,
    resid_ref,
    rows_ref,
    inner_ref,
    own_ref,
    sibling_ref,
    outgoing_ref,
    incoming_ref,
    small_sem,
    kv_sem,
    w_sem,
    ring_send,
    ring_recv,
    pair_send,
    pair_recv,
    back_pair_send,
    back_pair_recv,
    back_send,
    back_recv,
):
    chips = devices // 2
    hops = chips // 2
    count, width = hidden_ref.shape
    slots = keys_ref.shape[1]
    head_size = width // heads
    per_kv = heads // kv_heads
    half = count // 2
    top_count = ids_ref.shape[0]
    hidden_units = gate_ref.shape[1]

    me = lax.axis_index("ep")
    core = lax.rem(me, 2)
    position = position_of(me // 2, chips)
    right = chip_at(lax.rem(position + 1, chips), chips) * 2 + core
    left = chip_at(lax.rem(position + chips - 1, chips), chips) * 2 + core
    sibling = me + 1 - 2 * core
    onward = (right, left)

    small_copies = []
    for j, (src, dst) in enumerate(
        (
            (queries_hbm, queries_ref),
            (hidden_hbm, hidden_ref),
            (gain_hbm, gain_ref),
            (ids_hbm, ids_ref),
            (weights_hbm, weights_ref),
        )
    ):
        copy = pltpu.make_async_copy(src, dst, small_sem.at[j])
        copy.start()
        small_copies.append(copy)
    groups = count // GROUP
    kv_copies = []
    for i in range(groups):
        part = pl.ds(i * GROUP, GROUP)
        for j, (src, dst) in enumerate(((keys_hbm, keys_ref), (values_hbm, values_ref))):
            copy = pltpu.make_async_copy(src.at[part], dst.at[part], kv_sem.at[i, j])
            copy.start()
            kv_copies.append(copy)
    barrier = pltpu.get_barrier_semaphore()
    others = [left, right, sibling]
    for other in others:
        pl.semaphore_signal(
            barrier, inc=1, device_id={"ep": other}, device_id_type=pl.DeviceIdType.MESH
        )
    for copy in small_copies:
        copy.wait()

    scale = 1.0 / math.sqrt(head_size)
    square_rows = per_kv * GROUP
    row_id = lax.broadcasted_iota(jnp.int32, (square_rows, GROUP * slots), 0)
    col_id = lax.broadcasted_iota(jnp.int32, (square_rows, GROUP * slots), 1)
    column_request = col_id // slots
    same_request = (row_id % GROUP) == column_request
    slot_id = col_id % slots
    def attend(i):
        part = pl.ds(i * GROUP, GROUP)
        lengths = jnp.zeros((square_rows, GROUP * slots), jnp.int32)
        for r in range(GROUP):
            lengths = jnp.where(column_request == r, lengths_ref[i * GROUP + r], lengths)
        visible = same_request & (slot_id < lengths)
        group_queries = queries_ref[part, :].astype(jnp.float32)
        hidden = hidden_ref[part, :].astype(jnp.float32)
        for g in range(kv_heads):
            lanes = slice(g * head_size, (g + 1) * head_size)
            first = g * per_kv
            q = jnp.concatenate(
                [
                    group_queries[:, (first + h) * head_size : (first + h + 1) * head_size]
                    for h in range(per_kv)
                ],
                axis=0,
            ).astype(jnp.bfloat16)
            k = keys_ref[part, :, lanes].reshape(GROUP * slots, head_size)
            v = values_ref[part, :, lanes].reshape(GROUP * slots, head_size)
            scores = (
                lax.dot_general(q, k, (((1,), (1,)), ((), ())), preferred_element_type=jnp.float32)
                * scale
            )
            scores = jnp.where(visible, scores, -1e30)
            expo = jnp.exp(scores - jnp.max(scores, axis=-1, keepdims=True))
            probs = (expo * (1.0 / jnp.sum(expo, axis=-1, keepdims=True))).astype(jnp.bfloat16)
            attended = jnp.dot(probs, v, preferred_element_type=jnp.float32)
            for h in range(per_kv):
                cols = slice((first + h) * head_size, (first + h + 1) * head_size)
                resid_ref[part, cols] = hidden[:, cols] + attended[h * GROUP : (h + 1) * GROUP, :]

    spare = LANES - count
    ids = jnp.concatenate([ids_ref[...], jnp.zeros((top_count, spare), jnp.int32)], axis=1)
    weights = jnp.concatenate([weights_ref[...], jnp.zeros((top_count, spare), jnp.float32)], axis=1)
    expert_id = lax.broadcasted_iota(jnp.int32, (LANES, LANES), 0)
    turned = jnp.zeros((LANES, LANES), jnp.float32)
    for k in range(top_count):
        chosen = ids[k : k + 1, :]
        turned = turned + jnp.where(
            (expert_id == chosen) | (expert_id == chosen + devices), weights[k : k + 1, :], 0.0
        )
    table = turned.T[0:count, :]
    lane = lax.broadcasted_iota(jnp.int32, (count, LANES), 1)
    coarse = table.astype(jnp.bfloat16)
    fine = (table - coarse.astype(jnp.float32)).astype(jnp.bfloat16)
    rows_ref[0:count, width : width + LANES] = jnp.where(
        lane < devices, coarse.astype(jnp.float32), fine.astype(jnp.float32)
    ).astype(jnp.bfloat16)

    def normalize(h):
        part = pl.ds(h * half, half)
        resid = resid_ref[part, :]
        mean_square = jnp.mean(resid * resid, axis=-1, keepdims=True)
        rows_ref[part, 0:width] = (
            resid * lax.rsqrt(mean_square + 1e-06) * gain_ref[...]
        ).astype(jnp.bfloat16)

    def chunk(s):
        return 0 if s == 0 else 2 * count + (s - 1) * 4 * count

    def own_rows(s):
        return 0 if s == 0 else count + (s - 1) * 2 * count

    def half_at(s, direction, h):
        if s in (0, hops):
            return chunk(s) + h * half
        return chunk(s) + direction * count + h * half

    def remote(src, dst, send, recv, other):
        return pltpu.make_async_remote_copy(
            src_ref=src,
            dst_ref=dst,
            send_sem=send,
            recv_sem=recv,
            device_id={"ep": other},
            device_id_type=pl.DeviceIdType.MESH,
        )

    def travels(s, direction, h):
        return s < hops or h == direction

    split = width // 2 // LANES * LANES

    def part_of(c, end):
        return pl.ds(0, split) if c == 0 else pl.ds(split, end - split)

    def ring_copy(s, direction, h, c):
        cols = part_of(c, width + LANES)
        return remote(
            rows_ref.at[pl.ds(half_at(s - 1, direction, h), half), cols],
            rows_ref.at[pl.ds(half_at(s, direction, h), half), cols],
            ring_send.at[s - 1, direction, h, c],
            ring_recv.at[s - 1, direction, h, c],
            onward[direction],
        )

    def pair_copy(s, direction, h):
        start = half_at(s, direction, h)
        size = count if s in (0, hops) else 2 * count
        return remote(
            rows_ref.at[pl.ds(start, half)],
            rows_ref.at[pl.ds(start + size, half)],
            pair_send.at[s, direction, h],
            pair_recv.at[s, direction, h],
            sibling,
        )

    sent = []

    def go(copy):
        copy.start()
        sent.append(copy)

    def home(h):
        return pair_copy(0, 0, h)

    w_copies = []
    for h in range(2):
        for copy in kv_copies[h * groups : (h + 1) * groups]:
            copy.wait()
        for i in range(h * groups // 2, (h + 1) * groups // 2):
            attend(i)
        normalize(h)
        if h == 0:
            pl.semaphore_wait(barrier, len(others))
        for c in range(2):
            for direction in range(2):
                go(ring_copy(1, direction, h, c))
        go(home(h))
        if h == 0:
            for j, (src, dst) in enumerate(((gate_hbm, gate_ref), (up_hbm, up_ref), (down_hbm, down_ref))):
                copy = pltpu.make_async_copy(src.at[0], dst, w_sem.at[j])
                copy.start()
                w_copies.append(copy)

    f_tile = tile_of(hidden_units, 256)
    d_tile = tile_of(width, 512)

    def expert(start, size):
        span = pl.ds(start, size)

        def first(i):
            cols = slice(i * f_tile, (i + 1) * f_tile)
            x = rows_ref[span, 0:width]
            gate = jnp.dot(x, gate_ref[:, cols], preferred_element_type=jnp.float32)
            up = jnp.dot(x, up_ref[:, cols], preferred_element_type=jnp.float32)
            inner_ref[0:size, cols] = (gate / (1.0 + jnp.exp(-gate)) * up).astype(jnp.bfloat16)

        def second(i):
            cols = slice(i * d_tile, (i + 1) * d_tile)
            spot = lax.broadcasted_iota(jnp.int32, (size, LANES), 1)
            both = rows_ref[span, width : width + LANES].astype(jnp.float32)
            weight = jnp.sum(
                jnp.where((spot == me) | (spot == me + devices), both, 0.0), axis=-1, keepdims=True
            )
            result = jnp.dot(
                inner_ref[0:size, :], down_ref[:, cols], preferred_element_type=jnp.float32
            )
            own_ref[span, cols] = (result * weight).astype(jnp.bfloat16)

        steps = [functools.partial(first, i) for i in range(hidden_units // f_tile)]
        return steps + [functools.partial(second, i) for i in range(width // d_tile)]

    def back_pair(s, c):
        size = count if s in (0, hops) else 2 * count
        return remote(
            own_ref.at[pl.ds(chunk(s) + size, size), part_of(c, width)],
            sibling_ref.at[pl.ds(own_rows(s), size), part_of(c, width)],
            back_pair_send.at[s, c],
            back_pair_recv.at[s, c],
            sibling,
        )

    pending = []

    def run(amount):
        for _ in range(min(amount, len(pending))):
            pending.pop(0)()

    def arrived(s):
        if s == 0:
            for h in range(2):
                home(h).wait_recv()
        for h in range(2):
            for direction in range(2):
                if s > 0 and travels(s, direction, h):
                    pair_copy(s, direction, h).wait_recv()

    def work(first, last):
        for s in range(first, last + 1):
            arrived(s)
        end = chunk(last) + (2 if last in (0, hops) else 4) * count
        steps = expert(chunk(first), end - chunk(first))
        ready = hidden_units // f_tile - (-split // d_tile)
        for c, some in enumerate((steps[:ready], steps[ready:])):
            pending.extend(some)
            for s in range(first, last + 1):
                pending.append(lambda s=s, c=c: go(back_pair(s, c)))

    for s in range(1, hops + 1):
        for h in range(2):
            for c in range(2):
                for direction in range(2):
                    if travels(s, direction, h):
                        ring_copy(s, direction, h, c).wait_recv()
                        if s < hops and travels(s + 1, direction, h):
                            go(ring_copy(s + 1, direction, h, c))
                        if c == 1:
                            go(pair_copy(s, direction, h))
        if s == hops - 1:
            for copy in w_copies:
                copy.wait()
            for first in range(2, hops, 2):
                work(first, min(first + 1, hops - 1))
                run(len(pending))
    work(hops, hops)
    run(len(pending))
    work(0, 1)

    def back_copy(s, direction, h, c):
        spot = (direction, s - 1, pl.ds(h * half, half), part_of(c, width))
        return remote(
            outgoing_ref.at[spot],
            incoming_ref.at[spot],
            back_send.at[s - 1, direction, h, c],
            back_recv.at[s - 1, direction, h, c],
            onward[1 - direction],
        )

    def pass_back(s, direction, h, c):
        cols = part_of(c, width)
        start = half_at(s, direction, h)
        offset = start - chunk(s) + own_rows(s)
        total = own_ref[pl.ds(start, half), cols].astype(jnp.float32) + sibling_ref[
            pl.ds(offset, half), cols
        ].astype(jnp.float32)
        if s < hops and travels(s + 1, direction, h):
            back_copy(s + 1, direction, h, c).wait_recv()
            total = total + incoming_ref[direction, s, pl.ds(h * half, half), cols].astype(
                jnp.float32
            )
        outgoing_ref[direction, s - 1, pl.ds(h * half, half), cols] = total.astype(jnp.bfloat16)
        go(back_copy(s, direction, h, c))

    for s in range(hops, 0, -1):
        for c in range(2):
            if s == hops:
                back_pair(s, c).wait_recv()
            for direction in range(2):
                pass_back(s, direction, direction, c)
        if s > 1:
            if s == 2:
                run(len(pending))
            for c in range(2):
                back_pair(s - 1, c).wait_recv()
                for direction in range(2):
                    pass_back(s - 1, direction, 1 - direction, c)
            run(3)

    for c in range(2):
        back_pair(0, c).wait_recv()
    for h in range(2):
        span = pl.ds(h * half, half)
        total = own_ref[span, :].astype(jnp.float32) + sibling_ref[span, :].astype(jnp.float32)
        total = total + resid_ref[span, :]
        for direction in range(2):
            for c in range(2):
                back_copy(1, direction, h, c).wait_recv()
            total = total + incoming_ref[direction, 0, span, :].astype(jnp.float32)
        out_ref[span, :] = total

    for copy in sent:
        copy.wait_send()


def gathered_layer(
    hidden_in,
    queries,
    stored_keys,
    stored_values,
    stored_lengths,
    norm_gain,
    expert_ids,
    gate_weights,
    w_gate,
    w_up,
    w_down,
):
    devices = lax.axis_size("ep")
    count, width = hidden_in.shape
    hidden_units = w_gate.shape[2]
    hops = devices // 4
    vmem = pl.BlockSpec(memory_space=pltpu.VMEM)
    smem = pl.BlockSpec(memory_space=pltpu.SMEM)
    hbm = pl.BlockSpec(memory_space=pltpu.HBM)
    dma = pltpu.SemaphoreType.DMA
    bf16 = jnp.bfloat16
    top_count = expert_ids.shape[1]
    return pl.pallas_call(
        functools.partial(layer_kernel, devices, QUERY_HEADS, KEY_VALUE_HEADS),
        out_shape=jax.ShapeDtypeStruct((count, width), jnp.float32),
        in_specs=[hbm, hbm, smem] + [hbm] * 8,
        out_specs=vmem,
        scratch_shapes=[
            pltpu.VMEM((count, width), bf16),
            pltpu.VMEM((count, width), bf16),
            pltpu.VMEM((1, width), jnp.float32),
            pltpu.VMEM((top_count, count), jnp.int32),
            pltpu.VMEM((top_count, count), jnp.float32),
            pltpu.VMEM(stored_keys.shape, bf16),
            pltpu.VMEM(stored_values.shape, bf16),
            pltpu.VMEM(w_gate.shape[1:], bf16),
            pltpu.VMEM(w_up.shape[1:], bf16),
            pltpu.VMEM(w_down.shape[1:], bf16),
            pltpu.VMEM((count, width), jnp.float32),
            pltpu.VMEM((devices * count, width + LANES), bf16),
            pltpu.VMEM((8 * count, hidden_units), bf16),
            pltpu.VMEM((devices * count, width), bf16),
            pltpu.VMEM((devices * count // 2, width), bf16),
            pltpu.VMEM((2, hops, count, width), bf16),
            pltpu.VMEM((2, hops, count, width), bf16),
            dma((5,)),
            dma((count // GROUP, 2)),
            dma((3,)),
            dma((hops, 2, 2, 2)),
            dma((hops, 2, 2, 2)),
            dma((hops + 1, 2, 2)),
            dma((hops + 1, 2, 2)),
            dma((hops + 1, 2)),
            dma((hops + 1, 2)),
            dma((hops, 2, 2, 2)),
            dma((hops, 2, 2, 2)),
        ],
        compiler_params=pltpu.CompilerParams(
            collective_id=0, has_side_effects=True, vmem_limit_bytes=60 * 1024 * 1024
        ),
        name="gathered_layer",
    )(
        hidden_in,
        queries,
        stored_lengths,
        norm_gain[None, :],
        expert_ids.T,
        gate_weights.T,
        stored_keys,
        stored_values,
        w_gate,
        w_up,
        w_down,
    ).astype(bf16)


def gather_suits(devices, local_experts, count, top_count):
    return (
        local_experts == 1
        and devices % 8 == 0
        and 2 * devices <= LANES
        and count % 32 == 0
        and count <= LANES
        and 2 * top_count >= devices
    )


def local(
    hidden_in,
    queries,
    stored_keys,
    stored_values,
    stored_lengths,
    norm_gain,
    expert_ids,
    gate_weights,
    w_gate,
    w_up,
    w_down,
):
    devices = lax.axis_size("ep")
    if gather_suits(devices, w_gate.shape[0], hidden_in.shape[0], expert_ids.shape[1]):
        return gathered_layer(
            hidden_in,
            queries,
            stored_keys,
            stored_values,
            stored_lengths,
            norm_gain,
            expert_ids,
            gate_weights,
            w_gate,
            w_up,
            w_down,
        )
    experts = devices * w_gate.shape[0]
    top_count = expert_ids.shape[1]
    capacity = max(2, 3 * MB_ROWS * top_count // (2 * experts))
    return layer_rows(
        hidden_in,
        queries,
        stored_keys,
        stored_values,
        stored_lengths,
        norm_gain,
        expert_ids,
        gate_weights,
        w_gate,
        w_up,
        w_down,
        MB * capacity,
    )


def solution(mesh):
    in_specs = (
        P(("groups", "ep"), None),
        P(("groups", "ep"), None),
        P(("groups", "ep"), None, None),
        P(("groups", "ep"), None, None),
        P(("groups", "ep")),
        P(),
        P(("groups", "ep"), None),
        P(("groups", "ep"), None),
        P("ep", None, None),
        P("ep", None, None),
        P("ep", None, None),
    )
    out_specs = P(("groups", "ep"), None)
    return jax.shard_map(local, mesh=mesh, in_specs=in_specs, out_specs=out_specs, check_vma=False)
```
